32 devices in a mesh: ctx: 8 (over z, y), hg: 4 (over x, core).
Axes of the slice: x: 2, y: 2, z: 4, core: 2. Of those that a mesh axis runs over, the one named last changes fastest.
Arguments:
- doc_ids: int32 [4096], P('ctx'), may hold values from 0 to 7, never falling along the last dimension, each value on 1 to 1024 neighbouring positions
- rotated_queries: bfloat16 [4096, 2048], P('ctx', 'hg'), may hold values from -6 to 6
- rotated_keys: bfloat16 [4096, 512], P('ctx', 'hg'), may hold values from -6 to 6
- value_matrix: bfloat16 [4096, 512], P('ctx', 'hg'), may hold values from -6 to 6
- out_proj: bfloat16 [4096, 2048], P('ctx', 'hg'), may hold values from -0.125 to 0.125
- cotangent: bfloat16 [4096, 4096], P('ctx'), may hold values from -6 to 6
Outputs:
- layer_output: bfloat16 [4096, 4096], P('ctx', 'hg')
- query_grad: bfloat16 [4096, 2048], P('ctx', 'hg')
- key_gradient: bfloat16 [4096, 512], P('ctx', 'hg')
- value_gradient: bfloat16 [4096, 512], P('ctx', 'hg')
- proj_grad: bfloat16 [4096, 2048], P('ctx', 'hg')
The draws below stay inside these ranges and needn't reach their ends.
Inputs may be any that keep to these rules, and one draw needn't show every extreme that they name: `doc_ids`: document ids in token order, never falling; every document has 1 to 1024 tokens and one has exactly 1024.
All inputs are finite; a program needn't handle non-finite values.
Results may differ from the reference program's by a relative error of at most 0.013.
Values may be sent and summed in bfloat16 or wider, within the bound.
No kernel may reach another device: no remote copies, remote signals or barrier semaphores. Data moves between devices by JAX's collectives and lax.ppermute only.
A program may use at most 128 MiB of HBM per device.

```python
import math
import jax
import jax.numpy as jnp
import numpy as np
from jax import lax

D = 4096
QUERY_HEADS = 16
KEY_VALUE_HEADS = 4
HEAD_SIZE = 128
TOK_DEV = 512
CONTEXT_TOKENS = 4096
DOC_MOST = 1024
DOCS = 8


def starting_sample(key, salted, columns):
    folded = jax.random.fold_in(key, salted)
    return jax.random.truncated_normal(folded, -5.0, 5.0, (CONTEXT_TOKENS, columns), jnp.float32)


def draw_rotated_queries(key, part):
    sampled_items = starting_sample(key, 11, QUERY_HEADS * HEAD_SIZE)
    return sampled_items.astype(jnp.bfloat16)


def draw_rotated_keys(key, part):
    sampled_items = starting_sample(key, 13, KEY_VALUE_HEADS * HEAD_SIZE)
    return sampled_items.astype(jnp.bfloat16)


def with_spikes(values, stream_key, source, target, blocks, factor):
    def block_of(position):
        return (jnp.arange(values.shape[position]) // (values.shape[position] // blocks)).reshape((-1,) + (1,) * (values.ndim - 1 - position))

    near = jax.random.permutation(stream_key, blocks)[block_of(target)]
    far = (block_of(target) + blocks // 2) % blocks
    return jnp.where((block_of(source) == near) | (block_of(source) == far), factor * values, values)


def block_levels(key, extent, shards, low, high):
    loudness = 1.0
    for axis_at, shards_of in shards:
        steps = jax.random.uniform(jax.random.fold_in(jax.random.fold_in(key, 6), axis_at), (shards_of,), jnp.float32, low / len(shards), high / len(shards))
        loudness = loudness * jnp.repeat(jnp.exp(steps), extent[axis_at] // shards_of).reshape((-1,) + (1,) * (len(extent) - 1 - axis_at))
    return loudness


def length_profile(number_of, total, limit, slope):
    loads = [(1 << 20) // math.isqrt(rank ** slope) + 1 for rank in range(2, number_of + 1)]
    spare, holding = total - limit - (number_of - 1), [1] * (number_of - 1)
    while spare > 0:
        candidates = [i for i in range(number_of - 1) if holding[i] < limit]
        whole, remaining = sum([loads[i] for i in candidates]), spare
        for i in candidates:
            more = min(limit - holding[i], max(1, remaining * loads[i] // whole), spare)
            holding[i] = holding[i] + more
            spare = spare - more
    return np.array([limit] + holding)


def ragged_sizes(rng, number_of, total, most, slope):
    if number_of == 2:
        one = jax.random.randint(rng, (), max(1, total - most), min(most, total - 1) + 1)
        return jnp.stack([one, total - one])
    sizes = jnp.asarray(length_profile(number_of, total, most, slope), jnp.int32)
    couples = (number_of - 1) // 2
    donor, sink = sizes[1:1 + 2 * couples:2], sizes[2:2 + 2 * couples:2]
    slack = jnp.minimum(donor - 1, most - sink)
    passed = jax.random.randint(jax.random.fold_in(rng, 1), (couples,), 0, 1 << 20) % (slack + 1)
    sizes = sizes.at[1:1 + 2 * couples:2].set(donor - passed).at[2:2 + 2 * couples:2].set(sink + passed)
    return sizes[jax.random.permutation(jax.random.fold_in(rng, 2), number_of)]


def scatter_about(key, shape, spread, most, shards=(), kind=jnp.bfloat16):
    result = spread * jax.random.normal(key, shape, jnp.float32)
    if shards:
        result = result * block_levels(key, shape, shards, -0.22, 0.18)
    return jnp.clip(result, -most, most).astype(kind)


def bell_draw_with(rng, dims, width, most, split, heavy, kind=jnp.bfloat16):
    array = width * jax.random.normal(rng, dims, jnp.float32)
    if split:
        array = array * block_levels(rng, dims, split, -0.22, 0.18)
    return jnp.clip(with_spikes(array, jax.random.fold_in(rng, 3), *heavy), -most, most).astype(kind)


def setup_inputs(seed: int = 0) -> dict:
    splits = jax.random.split(jax.random.key(seed), 7)
    return {
        "doc_ids": jnp.searchsorted(jnp.cumsum(ragged_sizes(splits[0], DOCS, CONTEXT_TOKENS, DOC_MOST, 1)), jnp.arange(CONTEXT_TOKENS), side="right").astype(jnp.int32),
        "rotated_queries": draw_rotated_queries(jax.random.fold_in(splits[6], 71), 0),
        "rotated_keys": draw_rotated_keys(jax.random.fold_in(splits[6], 71), 0),
        "value_matrix": scatter_about(splits[3], (CONTEXT_TOKENS, KEY_VALUE_HEADS * HEAD_SIZE), 1.0, 6.0, ((0, 8), (1, 4))),
        "out_proj": scatter_about(splits[4], (D, QUERY_HEADS * HEAD_SIZE), (QUERY_HEADS * HEAD_SIZE) ** -0.5, 0.125, ((0, 8), (1, 4))),
        "cotangent": bell_draw_with(splits[5], (CONTEXT_TOKENS, D), 1.0, 6.0, ((0, 8),), (0, 1, 8, 2.0)),
    }


def reference(doc_ids, rotated_queries, rotated_keys, value_matrix, out_proj, cotangent):
    group_length = QUERY_HEADS // KEY_VALUE_HEADS
    score_scale = HEAD_SIZE ** -0.5
    block_rows = TOK_DEV
    block_count = CONTEXT_TOKENS // TOK_DEV
    border_amount = DOC_MOST
    window = DOC_MOST + TOK_DEV
    attention_gradient = jnp.dot(cotangent, out_proj, preferred_element_type=jnp.float32).astype(jnp.bfloat16)
    gradient_heads = attention_gradient.reshape(CONTEXT_TOKENS, KEY_VALUE_HEADS, group_length, HEAD_SIZE)
    query_head_list = rotated_queries.reshape(CONTEXT_TOKENS, KEY_VALUE_HEADS, group_length, HEAD_SIZE)
    padded_keys = jnp.concatenate([jnp.zeros((border_amount, KEY_VALUE_HEADS * HEAD_SIZE), jnp.bfloat16), rotated_keys], 0).reshape(CONTEXT_TOKENS + border_amount, KEY_VALUE_HEADS, HEAD_SIZE)
    padded_values = jnp.concatenate([jnp.zeros((border_amount, KEY_VALUE_HEADS * HEAD_SIZE), jnp.bfloat16), value_matrix], 0).reshape(CONTEXT_TOKENS + border_amount, KEY_VALUE_HEADS, HEAD_SIZE)
    pad_docs = jnp.concatenate([jnp.full((border_amount,), -1, jnp.int32), doc_ids.astype(jnp.int32)], 0)

    def one_block(carried, block_index):
        key_running_total, value_running_total = carried
        start_row = (block_index * block_rows).astype(jnp.int32)
        query_block = lax.dynamic_slice_in_dim(query_head_list, start_row, block_rows, 0).astype(jnp.float32)
        grad_block = lax.dynamic_slice_in_dim(gradient_heads, start_row, block_rows, 0).astype(jnp.float32)
        key_block = lax.dynamic_slice_in_dim(padded_keys, start_row, window, 0).astype(jnp.float32)
        value_block = lax.dynamic_slice_in_dim(padded_values, start_row, window, 0).astype(jnp.float32)
        query_docs = lax.dynamic_slice_in_dim(doc_ids.astype(jnp.int32), start_row, block_rows, 0)
        key_docs = lax.dynamic_slice_in_dim(pad_docs, start_row, window, 0)
        query_pos = start_row + jnp.arange(block_rows, dtype=jnp.int32)
        key_pos = start_row - border_amount + jnp.arange(window, dtype=jnp.int32)
        allowed = (query_docs[:, None] == key_docs[None, :]) & (key_pos[None, :] <= query_pos[:, None])
        scores = jnp.einsum("bkgd,wkd->kgbw", query_block, key_block) * score_scale
        masked = jnp.where(allowed, scores, -jnp.inf)
        row_max = jnp.max(masked, axis=3, keepdims=True)
        row_sum = jnp.sum(jnp.where(allowed, jnp.exp(masked - row_max), 0.0), axis=3, keepdims=True)
        log_total = row_max + jnp.log(row_sum)
        weights = jnp.where(allowed, jnp.exp(masked - log_total), 0.0)
        weights = lax.optimization_barrier(weights.astype(jnp.bfloat16)).astype(jnp.float32)
        attended = jnp.einsum("kgbw,wkd->bkgd", weights, value_block).astype(jnp.bfloat16)
        attended_wide = lax.optimization_barrier(attended).astype(jnp.float32)
        row_delta = jnp.einsum("bkgd,bkgd->kgb", grad_block, attended_wide)[..., None]
        grad_dots = jnp.einsum("bkgd,wkd->kgbw", grad_block, value_block)
        shifted = (weights * (grad_dots - row_delta) * score_scale).astype(jnp.bfloat16)
        shifted = lax.optimization_barrier(shifted).astype(jnp.float32)
        query_grad = jnp.einsum("kgbw,wkd->bkgd", shifted, key_block).astype(jnp.bfloat16)
        key_part = jnp.einsum("kgbw,bkgd->wkd", shifted, query_block)
        value_part = jnp.einsum("kgbw,bkgd->wkd", weights, grad_block)
        key_running_total = lax.dynamic_update_slice_in_dim(key_running_total, lax.dynamic_slice_in_dim(key_running_total, start_row, window, 0) + key_part, start_row, 0)
        value_running_total = lax.dynamic_update_slice_in_dim(value_running_total, lax.dynamic_slice_in_dim(value_running_total, start_row, window, 0) + value_part, start_row, 0)
        return (key_running_total, value_running_total), (attended, query_grad)

    zeroed_running_total = jnp.zeros((CONTEXT_TOKENS + border_amount, KEY_VALUE_HEADS, HEAD_SIZE), jnp.float32)
    (key_running_total, value_running_total), (attended, query_grad) = lax.scan(one_block, (zeroed_running_total, zeroed_running_total), jnp.arange(block_count, dtype=jnp.int32))
    attended = attended.reshape(CONTEXT_TOKENS, QUERY_HEADS * HEAD_SIZE)
    layer_output = jnp.dot(attended, out_proj.T, preferred_element_type=jnp.float32).astype(jnp.bfloat16)
    proj_grad = jnp.dot(cotangent.T, attended, preferred_element_type=jnp.float32).astype(jnp.bfloat16)
    query_grad = query_grad.reshape(CONTEXT_TOKENS, QUERY_HEADS * HEAD_SIZE)
    key_gradient = key_running_total[border_amount:].reshape(CONTEXT_TOKENS, KEY_VALUE_HEADS * HEAD_SIZE).astype(jnp.bfloat16)
    value_gradient = value_running_total[border_amount:].reshape(CONTEXT_TOKENS, KEY_VALUE_HEADS * HEAD_SIZE).astype(jnp.bfloat16)
    return (layer_output, query_grad, key_gradient, value_gradient, proj_grad)
```

```python
import functools

import jax
import jax.numpy as jnp
from jax import lax
from jax.experimental import pallas as pl
from jax.experimental.pallas import tpu as pltpu
from jax.sharding import PartitionSpec as P

HEAD_SIZE = 128
DOC_MOST = 1024
QUERY_TILE = 256
SCALE = HEAD_SIZE**-0.5
LOG2E = 1.4426950408889634
DOC_ROWS = 16


def dot_nn(a, b):
    return lax.dot_general(a, b, (((1,), (0,)), ((), ())), preferred_element_type=jnp.float32)


def dot_nt(a, b):
    return lax.dot_general(a, b, (((1,), (1,)), ((), ())), preferred_element_type=jnp.float32)


def dot_tn(a, b):
    return lax.dot_general(a, b, (((0,), (0,)), ((), ())), preferred_element_type=jnp.float32)


def windows(rows, key_rows):
    tile = min(QUERY_TILE, rows)
    for first in range(0, rows, tile):
        yield first, tile, first, DOC_MOST + tile


def mask_of(start_row, first, tile, low, width):
    key_pos = lax.broadcasted_iota(jnp.int32, (width, tile), 0) + low
    query_pos = lax.broadcasted_iota(jnp.int32, (width, tile), 1) + (first + DOC_MOST)
    return (key_pos <= query_pos) & (key_pos >= start_row)


def fill_keys(kv2, kv1, key_ref, value_ref, keys, values, rows):
    keys[0:rows] = kv2[0:rows, 0:HEAD_SIZE]
    keys[rows : 2 * rows] = kv1[0:rows, 0:HEAD_SIZE]
    keys[2 * rows : 3 * rows] = key_ref[...]
    values[0:rows] = kv2[0:rows, HEAD_SIZE:]
    values[rows : 2 * rows] = kv1[0:rows, HEAD_SIZE:]
    values[2 * rows : 3 * rows] = value_ref[...]


def forward_kernel(start, query, kv2, kv1, key_ref, value_ref, attended, log_total, keys, values):
    rows = query.shape[0]
    heads = query.shape[1] // HEAD_SIZE
    fill_keys(kv2, kv1, key_ref, value_ref, keys, values, rows)
    values_t = values[...].T
    for first, tile, low, width in windows(rows, keys.shape[0]):
        allowed = mask_of(start[:, first : first + tile], first, tile, low, width)
        for head in range(heads):
            lanes = slice(head * HEAD_SIZE, (head + 1) * HEAD_SIZE)
            scores = dot_nt(keys[low : low + width], query[first : first + tile, lanes])
            scores = jnp.where(allowed, scores * (SCALE * LOG2E), -jnp.inf)
            most = jnp.max(scores, axis=0, keepdims=True)
            weights = jnp.exp2(scores - most)
            total = jnp.sum(weights, axis=0, keepdims=True)
            out = dot_nn(values_t[:, low : low + width], weights.astype(jnp.bfloat16))
            attended[first : first + tile, lanes] = (out / total).T.astype(jnp.bfloat16)
            log_total[head : head + 1, first : first + tile] = most + jnp.log2(total)


def backward_kernel(
    start, log_total, query, kv2, kv1, key_ref, value_ref, attended, grad,
    query_grad, near, far, own, keys, values, key_sum, value_sum,
):
    rows = query.shape[0]
    heads = query.shape[1] // HEAD_SIZE
    fill_keys(kv2, kv1, key_ref, value_ref, keys, values, rows)
    keys_t = keys[...].T
    key_sum[...] = jnp.zeros_like(key_sum)
    value_sum[...] = jnp.zeros_like(value_sum)
    for first, tile, low, width in windows(rows, keys.shape[0]):
        allowed = mask_of(start[:, first : first + tile], first, tile, low, width)
        for head in range(heads):
            lanes = slice(head * HEAD_SIZE, (head + 1) * HEAD_SIZE)
            query_head = query[first : first + tile, lanes]
            grad_head = grad[first : first + tile, lanes]
            out_head = attended[first : first + tile, lanes]
            scores = dot_nt(keys[low : low + width], query_head) * (SCALE * LOG2E)
            scores = scores - log_total[head : head + 1, first : first + tile]
            weights = jnp.where(allowed, jnp.exp2(scores), 0.0)
            delta = grad_head.astype(jnp.float32) * out_head.astype(jnp.float32)
            delta = jnp.sum(delta.T, axis=0, keepdims=True)
            grad_dots = dot_nt(values[low : low + width], grad_head)
            shifted = (weights * (grad_dots - delta)).astype(jnp.bfloat16)
            value_sum[low : low + width] += dot_nn(weights.astype(jnp.bfloat16), grad_head)
            key_sum[low : low + width] += dot_nn(shifted, query_head)
            back = dot_nn(keys_t[:, low : low + width], shifted) * SCALE
            query_grad[first : first + tile, lanes] = back.T.astype(jnp.bfloat16)
    for place, out in enumerate((far, near, own)):
        part = slice(place * rows, (place + 1) * rows)
        out[:, 0:HEAD_SIZE] = (key_sum[part] * SCALE).astype(out.dtype)
        out[:, HEAD_SIZE:] = value_sum[part].astype(out.dtype)


def whole_vmem(count):
    return [pl.BlockSpec(memory_space=pltpu.VMEM)] * count


def params():
    return pltpu.CompilerParams(vmem_limit_bytes=48 * 1024 * 1024)


def attend(start, query, kv2, kv1, key, value):
    rows, columns = query.shape
    heads = columns // HEAD_SIZE
    cost = rows * (DOC_MOST + rows) * heads
    return pl.pallas_call(
        forward_kernel,
        out_shape=(
            jax.ShapeDtypeStruct((rows, columns), jnp.bfloat16),
            jax.ShapeDtypeStruct((heads, rows), jnp.float32),
        ),
        in_specs=whole_vmem(6),
        out_specs=tuple(whole_vmem(2)),
        scratch_shapes=[pltpu.VMEM((3 * rows, HEAD_SIZE), jnp.bfloat16)] * 2,
        compiler_params=params(),
        cost_estimate=pl.CostEstimate(flops=cost * 512, transcendentals=cost, bytes_accessed=4 * rows * columns),
        name="attend",
    )(start, query, kv2, kv1, key, value)


def attend_back(start, log_total, query, kv2, kv1, key, value, attended, grad):
    rows, columns = query.shape
    heads = columns // HEAD_SIZE
    cost = rows * (DOC_MOST + rows) * heads
    pair = jax.ShapeDtypeStruct((rows, 2 * HEAD_SIZE), jnp.bfloat16)
    return pl.pallas_call(
        backward_kernel,
        out_shape=(
            jax.ShapeDtypeStruct((rows, columns), jnp.bfloat16),
            pair,
            pair,
            jax.ShapeDtypeStruct((rows, 2 * HEAD_SIZE), jnp.float32),
        ),
        in_specs=whole_vmem(9),
        out_specs=tuple(whole_vmem(4)),
        scratch_shapes=[pltpu.VMEM((3 * rows, HEAD_SIZE), jnp.bfloat16)] * 2
        + [pltpu.VMEM((3 * rows, HEAD_SIZE), jnp.float32)] * 2,
        compiler_params=params(),
        cost_estimate=pl.CostEstimate(flops=cost * 1280, transcendentals=cost, bytes_accessed=10 * rows * columns),
        name="attend_back",
    )(start, log_total, query, kv2, kv1, key, value, attended, grad)


def swap_pair(value):
    devices = lax.axis_size("ctx")
    return lax.ppermute(value, "ctx", [(i, i ^ 1) for i in range(devices)])


def shift_line(value, by):
    devices = lax.axis_size("ctx")
    pairs = [(i, i + 2 * by) for i in range(devices) if 0 <= i + 2 * by < devices]
    return lax.ppermute(value, "ctx", pairs)


def swap_heads(value, bit):
    groups = lax.axis_size("hg")
    return lax.ppermute(value, "hg", [(i, i ^ bit) for i in range(groups)])


def line_pairs(pairs):
    return [(2 * a + y, 2 * b + y) for a, b in pairs for y in range(2)]


def along_line(value, pairs):
    return lax.ppermute(value, "ctx", line_pairs(pairs))


OUTER = [(0, 1), (1, 0), (2, 3), (3, 2)]
INNER = [(1, 2), (2, 1)]


def line_groups(line):
    return [[2 * i + y for i in range(line)] for y in range(2)]


def gather_line(value, line, place):
    if line != 4:
        return lax.all_gather(value, "ctx", axis=0, axis_index_groups=line_groups(line))
    end = (place == 0) | (place == 3)
    low = place < 2
    first = along_line(value, OUTER)
    second = along_line(value, INNER)
    third = along_line(first, INNER)
    fourth = along_line(second, OUTER)
    fifth = along_line(third, OUTER)
    near = jnp.where(end, fourth, second)
    far = jnp.where(end, fifth, third)
    even = jnp.where(place % 2 == 0, value, first)
    odd = jnp.where(place % 2 == 0, first, value)
    return jnp.stack([
        jnp.where(low, even, far),
        jnp.where(low, odd, near),
        jnp.where(low, near, even),
        jnp.where(low, far, odd),
    ])


def scatter_line(parts, line, place):
    if line != 4:
        return lax.psum_scatter(parts, "ctx", scatter_dimension=0, axis_index_groups=line_groups(line))
    order = jnp.array([[3, 2, 1, 0], [3, 2, 0, 1], [0, 1, 3, 2], [0, 1, 2, 3]], jnp.int32)[place]
    parts = [lax.dynamic_index_in_dim(parts, order[i], 0, keepdims=False) for i in range(4)]
    wide = [part.astype(jnp.float32) for part in parts]
    first = along_line(parts[0], OUTER)
    second = along_line(parts[1], OUTER)
    inner = along_line((wide[0] + first).astype(jnp.bfloat16), INNER)
    third = along_line((wide[2] + inner).astype(jnp.bfloat16), OUTER)
    other = along_line((wide[1] + second).astype(jnp.bfloat16), INNER)
    return wide[3] + third + other


def body(doc_ids, rotated_queries, rotated_keys, value_matrix, out_proj, cotangent):
    rows = rotated_queries.shape[0]
    columns = rotated_queries.shape[1]
    shard = out_proj.shape[0]
    devices = lax.axis_size("ctx")
    groups = lax.axis_size("hg")
    line = devices // 2
    index = lax.axis_index("ctx")
    parity, place = index % 2, index // 2
    group = lax.axis_index("hg")
    core, column = group % 2, group // 2
    half = line * shard

    kv = jnp.concatenate([rotated_keys, value_matrix], 1)
    docs = jnp.pad(doc_ids.reshape(-1, 2 * HEAD_SIZE), ((0, DOC_ROWS - rows // (2 * HEAD_SIZE)), (0, 0)))
    pack = jnp.concatenate([kv, docs.astype(jnp.bfloat16)], 0)
    far_kv = shift_line(pack, 1)
    near_kv = swap_pair(jnp.where(parity == 0, pack, far_kv))

    def docs_of(received, back):
        found = received[rows : rows + rows // (2 * HEAD_SIZE)].reshape(-1).astype(jnp.int32)
        return jnp.where(index >= back, found, -1)

    doc_window = jnp.concatenate([docs_of(far_kv, 2), docs_of(near_kv, 1), doc_ids])
    start = jnp.sum((doc_window[:, None] < doc_ids[None, :]).astype(jnp.int32), axis=0, keepdims=True)

    blocks = cotangent.reshape(rows, line, 2, shard)
    own_grad = lax.dynamic_index_in_dim(blocks, parity, 2, keepdims=False).reshape(rows, half)
    part = rows // groups
    sent = lax.dynamic_slice(blocks, (group * part, 0, 1 - parity, 0), (part, line, 1, shard)).reshape(part, half)
    quarter = swap_pair(sent)
    across = swap_heads(quarter, 2)
    mine = jnp.stack([jnp.where(column == 0, quarter, across), jnp.where(column == 0, across, quarter)])
    mate = swap_heads(mine, 1)
    pair_grad = jnp.stack([jnp.where(core == 0, mine, mate), jnp.where(core == 0, mate, mine)], 1)
    pair_grad = pair_grad.reshape(rows, half)

    weights = gather_line(out_proj, line, place).reshape(half, columns)

    attended, log_total = attend(start, rotated_queries, far_kv, near_kv, rotated_keys, value_matrix)
    pair_attended = swap_pair(attended)

    proj_parts = (dot_tn(own_grad, attended) + dot_tn(pair_grad, pair_attended)).astype(jnp.bfloat16)
    proj_grad = scatter_line(proj_parts.reshape(line, shard, columns), line, place).astype(jnp.bfloat16)

    pair_part = swap_pair(dot_nn(pair_grad, weights).astype(jnp.bfloat16))
    grad = (dot_nn(own_grad, weights) + pair_part).astype(jnp.bfloat16)

    width = half // groups
    chunks = weights.reshape(2, 2, width, columns)

    def chunk_of(across_at, core_at):
        return lax.dynamic_slice(chunks, (across_at, core_at, 0, 0), (1, 1, width, columns)).reshape(width, columns)

    order = [chunk_of(1 - column, 1 - core), chunk_of(column, 1 - core), chunk_of(1 - column, core), chunk_of(column, core)]

    def reduced(tokens):
        parts = [dot_nt(tokens, item) for item in order]
        mates = swap_heads(jnp.stack(parts[0:2]).astype(jnp.bfloat16), 1)
        across = swap_heads((parts[2] + mates[0]).astype(jnp.bfloat16), 2)
        return (parts[3] + mates[1] + across).astype(jnp.bfloat16)

    other_part = swap_pair(reduced(pair_attended))
    own_part = reduced(attended)
    layer_output = jnp.stack([
        jnp.where(parity == 0, own_part, other_part).reshape(rows, -1, shard),
        jnp.where(parity == 0, other_part, own_part).reshape(rows, -1, shard),
    ], 2).reshape(rows, 2 * width)

    query_grad, near, far, own = attend_back(
        start, log_total, rotated_queries, far_kv, near_kv, rotated_keys, value_matrix, attended, grad
    )
    returned = swap_pair(near)
    passed = far.astype(jnp.float32) + jnp.where(parity == 1, returned, 0)
    arrived = shift_line(passed.astype(jnp.bfloat16), -1)
    own = own + arrived + jnp.where(parity == 0, returned, 0)
    own = own.astype(jnp.bfloat16)
    return (layer_output, query_grad, own[:, 0:HEAD_SIZE], own[:, HEAD_SIZE:], proj_grad)


def solution(mesh):
    split = P("ctx", "hg")
    in_specs = (P("ctx"), split, split, split, split, P("ctx", None))
    return jax.shard_map(body, mesh=mesh, in_specs=in_specs, out_specs=(split,) * 5, check_vma=False)
```

```python
import functools

import jax
import jax.numpy as jnp
from jax import lax
from jax.experimental import pallas as pl
from jax.experimental.pallas import tpu as pltpu
from jax.sharding import PartitionSpec as P

HEAD_SIZE = 128
DOC_MOST = 1024
QUERY_TILE = 256
SCALE = HEAD_SIZE**-0.5
LOG2E = 1.4426950408889634
DOC_ROWS = 16


def dot_nn(a, b):
    return lax.dot_general(a, b, (((1,), (0,)), ((), ())), preferred_element_type=jnp.float32)


def dot_nt(a, b):
    return lax.dot_general(a, b, (((1,), (1,)), ((), ())), preferred_element_type=jnp.float32)


def dot_tn(a, b):
    return lax.dot_general(a, b, (((0,), (0,)), ((), ())), preferred_element_type=jnp.float32)


def windows(rows, key_rows):
    tile = min(QUERY_TILE, rows)
    for first in range(0, rows, tile):
        yield first, tile, first, DOC_MOST + tile


def mask_of(start_row, first, tile, low, width):
    key_pos = lax.broadcasted_iota(jnp.int32, (width, tile), 0) + low
    query_pos = lax.broadcasted_iota(jnp.int32, (width, tile), 1) + (first + DOC_MOST)
    return (key_pos <= query_pos) & (key_pos >= start_row)


def fill_keys(kv2, kv1, key_ref, value_ref, keys, values, rows):
    keys[0:rows] = kv2[0:rows, 0:HEAD_SIZE]
    keys[rows : 2 * rows] = kv1[0:rows, 0:HEAD_SIZE]
    keys[2 * rows : 3 * rows] = key_ref[...]
    values[0:rows] = kv2[0:rows, HEAD_SIZE:]
    values[rows : 2 * rows] = kv1[0:rows, HEAD_SIZE:]
    values[2 * rows : 3 * rows] = value_ref[...]


def forward_kernel(start, query, kv2, kv1, key_ref, value_ref, attended, log_total, keys, values):
    rows = query.shape[0]
    heads = query.shape[1] // HEAD_SIZE
    fill_keys(kv2, kv1, key_ref, value_ref, keys, values, rows)
    values_t = values[...].T
    for first, tile, low, width in windows(rows, keys.shape[0]):
        allowed = mask_of(start[:, first : first + tile], first, tile, low, width)
        for head in range(heads):
            lanes = slice(head * HEAD_SIZE, (head + 1) * HEAD_SIZE)
            scores = dot_nt(keys[low : low + width], query[first : first + tile, lanes])
            scores = jnp.where(allowed, scores * (SCALE * LOG2E), -jnp.inf)
            most = jnp.max(scores, axis=0, keepdims=True)
            weights = jnp.exp2(scores - most)
            total = jnp.sum(weights, axis=0, keepdims=True)
            out = dot_nn(values_t[:, low : low + width], weights.astype(jnp.bfloat16))
            attended[first : first + tile, lanes] = (out / total).T.astype(jnp.bfloat16)
            log_total[head : head + 1, first : first + tile] = most + jnp.log2(total)


def backward_kernel(
    start, log_total, query, kv2, kv1, key_ref, value_ref, attended, own_grad, pair_grad,
    query_grad, near, far, own, keys, values, key_sum, value_sum, grad,
):
    rows = query.shape[0]
    heads = query.shape[1] // HEAD_SIZE
    fill_keys(kv2, kv1, key_ref, value_ref, keys, values, rows)
    keys_t = keys[...].T
    grad[...] = (own_grad[...] + pair_grad[...]).astype(grad.dtype)
    key_sum[...] = jnp.zeros_like(key_sum)
    value_sum[...] = jnp.zeros_like(value_sum)
    for first, tile, low, width in windows(rows, keys.shape[0]):
        allowed = mask_of(start[:, first : first + tile], first, tile, low, width)
        for head in range(heads):
            lanes = slice(head * HEAD_SIZE, (head + 1) * HEAD_SIZE)
            query_head = query[first : first + tile, lanes]
            grad_head = grad[first : first + tile, lanes]
            out_head = attended[first : first + tile, lanes]
            scores = dot_nt(keys[low : low + width], query_head) * (SCALE * LOG2E)
            scores = scores - log_total[head : head + 1, first : first + tile]
            weights = jnp.where(allowed, jnp.exp2(scores), 0.0)
            delta = grad_head.astype(jnp.float32) * out_head.astype(jnp.float32)
            delta = jnp.sum(delta.T, axis=0, keepdims=True)
            grad_dots = dot_nt(values[low : low + width], grad_head)
            shifted = (weights * (grad_dots - delta)).astype(jnp.bfloat16)
            value_sum[low : low + width] += dot_nn(weights.astype(jnp.bfloat16), grad_head)
            key_sum[low : low + width] += dot_nn(shifted, query_head)
            back = dot_nn(keys_t[:, low : low + width], shifted) * SCALE
            query_grad[first : first + tile, lanes] = back.T.astype(jnp.bfloat16)
    for place, out in enumerate((far, near, own)):
        part = slice(place * rows, (place + 1) * rows)
        out[:, 0:HEAD_SIZE] = (key_sum[part] * SCALE).astype(out.dtype)
        out[:, HEAD_SIZE:] = value_sum[part].astype(out.dtype)


def whole_vmem(count):
    return [pl.BlockSpec(memory_space=pltpu.VMEM)] * count


def params():
    return pltpu.CompilerParams(vmem_limit_bytes=48 * 1024 * 1024)


def attend(start, query, kv2, kv1, key, value):
    rows, columns = query.shape
    heads = columns // HEAD_SIZE
    cost = rows * (DOC_MOST + rows) * heads
    return pl.pallas_call(
        forward_kernel,
        out_shape=(
            jax.ShapeDtypeStruct((rows, columns), jnp.bfloat16),
            jax.ShapeDtypeStruct((heads, rows), jnp.float32),
        ),
        in_specs=whole_vmem(6),
        out_specs=tuple(whole_vmem(2)),
        scratch_shapes=[pltpu.VMEM((3 * rows, HEAD_SIZE), jnp.bfloat16)] * 2,
        compiler_params=params(),
        cost_estimate=pl.CostEstimate(flops=cost * 512, transcendentals=cost, bytes_accessed=4 * rows * columns),
        name="attend",
    )(start, query, kv2, kv1, key, value)


def attend_back(start, log_total, query, kv2, kv1, key, value, attended, own_grad, pair_grad):
    rows, columns = query.shape
    heads = columns // HEAD_SIZE
    cost = rows * (DOC_MOST + rows) * heads
    pair = jax.ShapeDtypeStruct((rows, 2 * HEAD_SIZE), jnp.bfloat16)
    return pl.pallas_call(
        backward_kernel,
        out_shape=(
            jax.ShapeDtypeStruct((rows, columns), jnp.bfloat16),
            pair,
            pair,
            jax.ShapeDtypeStruct((rows, 2 * HEAD_SIZE), jnp.float32),
        ),
        in_specs=whole_vmem(10),
        out_specs=tuple(whole_vmem(4)),
        scratch_shapes=[pltpu.VMEM((3 * rows, HEAD_SIZE), jnp.bfloat16)] * 2
        + [pltpu.VMEM((3 * rows, HEAD_SIZE), jnp.float32)] * 2
        + [pltpu.VMEM((rows, columns), jnp.bfloat16)],
        compiler_params=params(),
        cost_estimate=pl.CostEstimate(flops=cost * 1280, transcendentals=cost, bytes_accessed=10 * rows * columns),
        name="attend_back",
    )(start, log_total, query, kv2, kv1, key, value, attended, own_grad, pair_grad)


def output_kernel(order, tokens, weights, sent, far, near):
    sent[0] = dot_nt(tokens[...], weights[order[0]]).astype(sent.dtype)
    sent[1] = dot_nt(tokens[...], weights[order[1]]).astype(sent.dtype)
    far[...] = dot_nt(tokens[...], weights[order[2]]).astype(far.dtype)
    near[...] = dot_nt(tokens[...], weights[order[3]]).astype(near.dtype)


def output_parts_of(order, tokens, weights):
    line, shard, columns = weights.shape
    rows = tokens.shape[0]
    return pl.pallas_call(
        output_kernel,
        out_shape=(
            jax.ShapeDtypeStruct((2, rows, shard), jnp.bfloat16),
            jax.ShapeDtypeStruct((rows, shard), jnp.float32),
            jax.ShapeDtypeStruct((rows, shard), jnp.float32),
        ),
        in_specs=[pl.BlockSpec(memory_space=pltpu.SMEM)] + whole_vmem(2),
        out_specs=tuple(whole_vmem(3)),
        compiler_params=params(),
        cost_estimate=pl.CostEstimate(
            flops=2 * line * shard * rows * columns, transcendentals=0, bytes_accessed=8 * line * shard * rows
        ),
        name="output_parts",
    )(order, tokens, weights)


def swap_pair(value):
    devices = lax.axis_size("ctx")
    return lax.ppermute(value, "ctx", [(i, i ^ 1) for i in range(devices)])


def shift_line(value, by):
    devices = lax.axis_size("ctx")
    pairs = [(i, i + 2 * by) for i in range(devices) if 0 <= i + 2 * by < devices]
    return lax.ppermute(value, "ctx", pairs)


def swap_heads(value, bit):
    groups = lax.axis_size("hg")
    return lax.ppermute(value, "hg", [(i, i ^ bit) for i in range(groups)])


def line_pairs(pairs):
    return [(2 * a + y, 2 * b + y) for a, b in pairs for y in range(2)]


def along_line(value, pairs):
    return lax.ppermute(value, "ctx", line_pairs(pairs))


OUTER = [(0, 1), (1, 0), (2, 3), (3, 2)]
INNER = [(1, 2), (2, 1)]


def line_groups(line):
    return [[2 * i + y for i in range(line)] for y in range(2)]


def after(value, *others):
    return lax.optimization_barrier((value, *others))[0]


def scatter_four(parts):
    wide = [part.astype(jnp.float32) for part in parts]
    first = along_line(parts[0], OUTER)
    second = along_line(parts[1], OUTER)
    inner = along_line((wide[0] + first).astype(jnp.bfloat16), INNER)
    third = along_line((wide[2] + inner).astype(jnp.bfloat16), OUTER)
    other = along_line((wide[1] + second).astype(jnp.bfloat16), INNER)
    return (wide[3] + third + other).astype(jnp.bfloat16)


def body(doc_ids, rotated_queries, rotated_keys, value_matrix, out_proj, cotangent):
    rows = rotated_queries.shape[0]
    columns = rotated_queries.shape[1]
    shard = out_proj.shape[0]
    devices = lax.axis_size("ctx")
    groups = lax.axis_size("hg")
    line = devices // 2
    index = lax.axis_index("ctx")
    parity, place = index % 2, index // 2
    group = lax.axis_index("hg")

    kv = jnp.concatenate([rotated_keys, value_matrix], 1)
    docs = jnp.pad(doc_ids.reshape(-1, 2 * HEAD_SIZE), ((0, DOC_ROWS - rows // (2 * HEAD_SIZE)), (0, 0)))
    pack = jnp.concatenate([kv, docs.astype(jnp.bfloat16)], 0)
    far_kv = shift_line(pack, 1)

    fast = line == 4 and groups == 4 and shard % HEAD_SIZE == 0
    low = place < 2
    order = [jnp.where(low, 3, 0), jnp.where(low, 2, 1), place ^ 1, place] if fast else list(range(line))
    part = rows // groups

    def columns_of(value, row, count, kind):
        return jnp.concatenate([
            lax.dynamic_slice(value, (row, (2 * order[i] + kind) * shard), (count, shard)) for i in range(line)
        ], 1)

    sent = columns_of(after(cotangent, pack), group * part, part, 1 - parity)
    quarter = swap_pair(sent)
    out_proj, cotangent = after(out_proj, sent), after(cotangent, sent)
    blocks = columns_of(cotangent, 0, rows, parity)

    relay = jnp.where(parity == 0, pack, after(far_kv, blocks))
    near_kv = swap_pair(relay)

    def docs_of(received, back):
        found = received[rows : rows + rows // (2 * HEAD_SIZE)].reshape(-1).astype(jnp.int32)
        return jnp.where(index >= back, found, -1)

    doc_window = jnp.concatenate([docs_of(far_kv, 2), docs_of(near_kv, 1), doc_ids])
    start = jnp.sum((doc_window[:, None] < doc_ids[None, :]).astype(jnp.int32), axis=0, keepdims=True)

    if fast:
        first = along_line(out_proj, OUTER)
        second = along_line(out_proj, INNER)
        quarter = after(quarter, relay)
        first, second = after(first, quarter), after(second, quarter)
        near_kv = after(near_kv, first, second)
        third = along_line(first, INNER)
        fourth = along_line(second, OUTER)
        fifth = along_line(third, OUTER)
        end = (place == 0) | (place == 3)
    else:
        weights = lax.all_gather(out_proj, "ctx", axis=0, axis_index_groups=line_groups(line)).reshape(-1, columns)

    attended, log_total = attend(start, rotated_queries, far_kv, near_kv, rotated_keys, value_matrix)
    pair_attended = swap_pair(attended)

    across = swap_heads(quarter, 2)
    mates = swap_heads(jnp.stack([quarter, across]), 1)
    pair_blocks = jnp.zeros_like(blocks)
    for piece, owner in ((quarter, group), (across, group ^ 2), (mates[0], group ^ 1), (mates[1], group ^ 3)):
        pair_blocks = lax.dynamic_update_slice(pair_blocks, piece, (owner * part, 0))

    proj_parts = (dot_tn(blocks, attended) + dot_tn(pair_blocks, pair_attended)).astype(jnp.bfloat16)
    proj_parts = proj_parts.reshape(line, shard, columns)
    if fast:
        proj_grad = scatter_four([proj_parts[i] for i in range(line)])
        near_half = jnp.concatenate([first, out_proj], 0)
        far_half = jnp.concatenate([jnp.where(end, fifth, third), jnp.where(end, fourth, second)], 0)
        near_half = after(near_half, proj_parts)
        pair_part = dot_nn(pair_blocks[:, 2 * shard :], near_half) + dot_nn(pair_blocks[:, : 2 * shard], far_half)
        weights = jnp.concatenate([far_half, near_half], 0)
    else:
        proj_grad = lax.psum_scatter(proj_parts, "ctx", scatter_dimension=0, axis_index_groups=line_groups(line))
        pair_part = dot_nn(pair_blocks, weights)
    pair_part = pair_part.astype(jnp.bfloat16)
    pair_attended, weights = lax.optimization_barrier((pair_attended, weights, pair_part))[0:2]
    pair_part = swap_pair(pair_part)
    own_part = dot_nn(blocks, weights)
    weights = weights.reshape(line, shard, columns)

    ways = [group ^ 3, group ^ 1, group ^ 2, group]

    slots = jnp.stack([sum(jnp.where(order[i] == way, i, 0) for i in range(line)) for way in ways]).astype(jnp.int32)

    def reduced(tokens):
        if fast:
            sent, far, near = output_parts_of(slots, tokens, weights)
        else:
            chunks = weights.reshape(groups, -1, columns)
            items = [lax.dynamic_index_in_dim(chunks, way, 0, keepdims=False) for way in ways]
            parts = [dot_nt(tokens, item) for item in items]
            sent, far, near = jnp.stack(parts[0:2]).astype(jnp.bfloat16), parts[2], parts[3]
        mates = swap_heads(sent, 1)
        across = swap_heads((far + mates[0]).astype(jnp.bfloat16), 2)
        return (near + mates[1] + across).astype(jnp.bfloat16)

    other_output = swap_pair(reduced(pair_attended))
    own_output = reduced(attended)
    layer_output = jnp.stack([
        jnp.where(parity == 0, own_output, other_output).reshape(rows, -1, shard),
        jnp.where(parity == 0, other_output, own_output).reshape(rows, -1, shard),
    ], 2).reshape(rows, -1)

    query_grad, near, far, own = attend_back(
        start, log_total, rotated_queries, far_kv, near_kv, rotated_keys, value_matrix, attended, own_part, pair_part
    )
    returned = swap_pair(near)
    passed = far.astype(jnp.float32) + jnp.where(parity == 1, returned, 0)
    arrived = shift_line(passed.astype(jnp.bfloat16), -1)
    own = own + arrived + jnp.where(parity == 0, returned, 0)
    own = own.astype(jnp.bfloat16)
    return (layer_output, query_grad, own[:, 0:HEAD_SIZE], own[:, HEAD_SIZE:], proj_grad)


def solution(mesh):
    split = P("ctx", "hg")
    in_specs = (P("ctx"), split, split, split, split, P("ctx", None))
    return jax.shard_map(body, mesh=mesh, in_specs=in_specs, out_specs=(split,) * 5, check_vma=False)
```

```python
import functools

import jax
import jax.numpy as jnp
from jax import lax
from jax.experimental import pallas as pl
from jax.experimental.pallas import tpu as pltpu
from jax.sharding import PartitionSpec as P

HEAD_SIZE = 128
DOC_MOST = 1024
QUERY_TILE = 256
SCALE = HEAD_SIZE**-0.5
LOG2E = 1.4426950408889634
DOC_ROWS = 16
OPT = dict(bwd='sent0', chunks='far_half', mates='', ownearly=1, pa='', passed='')


def dot_nn(a, b):
    return lax.dot_general(a, b, (((1,), (0,)), ((), ())), preferred_element_type=jnp.float32)


def dot_nt(a, b):
    return lax.dot_general(a, b, (((1,), (1,)), ((), ())), preferred_element_type=jnp.float32)


def dot_tn(a, b):
    return lax.dot_general(a, b, (((0,), (0,)), ((), ())), preferred_element_type=jnp.float32)


def windows(rows, key_rows):
    tile = min(QUERY_TILE, rows)
    for first in range(0, rows, tile):
        yield first, tile, first, DOC_MOST + tile


def mask_of(start_row, first, tile, low, width):
    key_pos = lax.broadcasted_iota(jnp.int32, (width, tile), 0) + low
    query_pos = lax.broadcasted_iota(jnp.int32, (width, tile), 1) + (first + DOC_MOST)
    return (key_pos <= query_pos) & (key_pos >= start_row)


def fill_keys(kv2, kv1, key_ref, value_ref, keys, values, rows):
    keys[0:rows] = kv2[0:rows, 0:HEAD_SIZE]
    keys[rows : 2 * rows] = kv1[0:rows, 0:HEAD_SIZE]
    keys[2 * rows : 3 * rows] = key_ref[...]
    values[0:rows] = kv2[0:rows, HEAD_SIZE:]
    values[rows : 2 * rows] = kv1[0:rows, HEAD_SIZE:]
    values[2 * rows : 3 * rows] = value_ref[...]


def forward_kernel(start, query, kv2, kv1, key_ref, value_ref, attended, log_total, keys, values):
    rows = query.shape[0]
    heads = query.shape[1] // HEAD_SIZE
    fill_keys(kv2, kv1, key_ref, value_ref, keys, values, rows)
    values_t = values[...].T
    for first, tile, low, width in windows(rows, keys.shape[0]):
        allowed = mask_of(start[:, first : first + tile], first, tile, low, width)
        for head in range(heads):
            lanes = slice(head * HEAD_SIZE, (head + 1) * HEAD_SIZE)
            scores = dot_nt(keys[low : low + width], query[first : first + tile, lanes])
            scores = jnp.where(allowed, scores * (SCALE * LOG2E), -jnp.inf)
            most = jnp.max(scores, axis=0, keepdims=True)
            weights = jnp.exp2(scores - most)
            total = jnp.sum(weights, axis=0, keepdims=True)
            out = dot_nn(values_t[:, low : low + width], weights.astype(jnp.bfloat16))
            attended[first : first + tile, lanes] = (out / total).T.astype(jnp.bfloat16)
            log_total[head : head + 1, first : first + tile] = most + jnp.log2(total)


def backward_kernel(
    start, log_total, query, kv2, kv1, key_ref, value_ref, attended, own_grad, pair_grad,
    query_grad, near, far, own, keys, values, key_sum, value_sum, grad,
):
    rows = query.shape[0]
    heads = query.shape[1] // HEAD_SIZE
    fill_keys(kv2, kv1, key_ref, value_ref, keys, values, rows)
    keys_t = keys[...].T
    grad[...] = (own_grad[...] + pair_grad[...]).astype(grad.dtype)
    key_sum[...] = jnp.zeros_like(key_sum)
    value_sum[...] = jnp.zeros_like(value_sum)
    for first, tile, low, width in windows(rows, keys.shape[0]):
        allowed = mask_of(start[:, first : first + tile], first, tile, low, width)
        for head in range(heads):
            lanes = slice(head * HEAD_SIZE, (head + 1) * HEAD_SIZE)
            query_head = query[first : first + tile, lanes]
            grad_head = grad[first : first + tile, lanes]
            out_head = attended[first : first + tile, lanes]
            scores = dot_nt(keys[low : low + width], query_head) * (SCALE * LOG2E)
            scores = scores - log_total[head : head + 1, first : first + tile]
            weights = jnp.where(allowed, jnp.exp2(scores), 0.0)
            delta = grad_head.astype(jnp.float32) * out_head.astype(jnp.float32)
            delta = jnp.sum(delta.T, axis=0, keepdims=True)
            grad_dots = dot_nt(values[low : low + width], grad_head)
            shifted = (weights * (grad_dots - delta)).astype(jnp.bfloat16)
            value_sum[low : low + width] += dot_nn(weights.astype(jnp.bfloat16), grad_head)
            key_sum[low : low + width] += dot_nn(shifted, query_head)
            back = dot_nn(keys_t[:, low : low + width], shifted) * SCALE
            query_grad[first : first + tile, lanes] = back.T.astype(jnp.bfloat16)
    for place, out in enumerate((far, near, own)):
        part = slice(place * rows, (place + 1) * rows)
        out[:, 0:HEAD_SIZE] = (key_sum[part] * SCALE).astype(out.dtype)
        out[:, HEAD_SIZE:] = value_sum[part].astype(out.dtype)


def whole_vmem(count):
    return [pl.BlockSpec(memory_space=pltpu.VMEM)] * count


def params(megabytes):
    return pltpu.CompilerParams(vmem_limit_bytes=megabytes * 1024 * 1024)


def attend(start, query, kv2, kv1, key, value):
    rows, columns = query.shape
    heads = columns // HEAD_SIZE
    cost = rows * (DOC_MOST + rows) * heads
    return pl.pallas_call(
        forward_kernel,
        out_shape=(
            jax.ShapeDtypeStruct((rows, columns), jnp.bfloat16),
            jax.ShapeDtypeStruct((heads, rows), jnp.float32),
        ),
        in_specs=whole_vmem(6),
        out_specs=tuple(whole_vmem(2)),
        scratch_shapes=[pltpu.VMEM((3 * rows, HEAD_SIZE), jnp.bfloat16)] * 2,
        compiler_params=params(OPT.get('vm_f', 16)),
        cost_estimate=pl.CostEstimate(flops=cost * 512, transcendentals=cost, bytes_accessed=4 * rows * columns),
        name="attend",
    )(start, query, kv2, kv1, key, value)


def attend_back(start, log_total, query, kv2, kv1, key, value, attended, own_grad, pair_grad):
    rows, columns = query.shape
    heads = columns // HEAD_SIZE
    cost = rows * (DOC_MOST + rows) * heads
    pair = jax.ShapeDtypeStruct((rows, 2 * HEAD_SIZE), jnp.bfloat16)
    return pl.pallas_call(
        backward_kernel,
        out_shape=(
            jax.ShapeDtypeStruct((rows, columns), jnp.bfloat16),
            pair,
            pair,
            jax.ShapeDtypeStruct((rows, 2 * HEAD_SIZE), jnp.float32),
        ),
        in_specs=whole_vmem(10),
        out_specs=tuple(whole_vmem(4)),
        scratch_shapes=[pltpu.VMEM((3 * rows, HEAD_SIZE), jnp.bfloat16)] * 2
        + [pltpu.VMEM((3 * rows, HEAD_SIZE), jnp.float32)] * 2
        + [pltpu.VMEM((rows, columns), jnp.bfloat16)],
        compiler_params=params(OPT.get('vm_b', 24)),
        cost_estimate=pl.CostEstimate(flops=cost * 1280, transcendentals=cost, bytes_accessed=10 * rows * columns),
        name="attend_back",
    )(start, log_total, query, kv2, kv1, key, value, attended, own_grad, pair_grad)


def output_kernel(slots, tokens, late, early, sent, kept):
    shard = sent.shape[2]
    for weights, own, role in ((early, slots[0], slots[2]), (late, slots[1], 1 - slots[2])):
        for row, out in ((1 - own, sent), (own, kept)):
            rows = pl.ds(pl.multiple_of(row * shard, shard), shard)
            out[role] = dot_nt(tokens[...], weights[rows]).astype(out.dtype)


def output_parts_of(slots, tokens, late, early):
    shard, columns = early.shape[0] // 2, early.shape[1]
    rows = tokens.shape[0]
    result = jax.ShapeDtypeStruct((2, rows, shard), jnp.bfloat16)
    return pl.pallas_call(
        output_kernel,
        out_shape=(result, result),
        in_specs=[pl.BlockSpec(memory_space=pltpu.SMEM)] + whole_vmem(3),
        out_specs=tuple(whole_vmem(2)),
        compiler_params=params(OPT.get("vm_out", 12)),
        cost_estimate=pl.CostEstimate(
            flops=8 * shard * rows * columns, transcendentals=0, bytes_accessed=32 * shard * rows
        ),
        name="output_parts",
    )(slots, tokens, late, early)


def swap_pair(value):
    devices = lax.axis_size("ctx")
    return lax.ppermute(value, "ctx", [(i, i ^ 1) for i in range(devices)])


def shift_line(value, by):
    if by < 0 and OPT.get("open", 0):
        devices = lax.axis_size("ctx")
        return lax.ppermute(value, "ctx", [(i, i + 2 * by) for i in range(devices) if i + 2 * by >= 0])
    devices = lax.axis_size("ctx")
    return lax.ppermute(value, "ctx", [(i, (i + 2 * by) % devices) for i in range(devices)])


def swap_heads(value, bit):
    groups = lax.axis_size("hg")
    return lax.ppermute(value, "hg", [(i, i ^ bit) for i in range(groups)])


def line_pairs(pairs):
    return [(2 * a + y, 2 * b + y) for a, b in pairs for y in range(2)]


def along_line(value, pairs):
    return lax.ppermute(value, "ctx", line_pairs(pairs))


OUTER = [(0, 1), (1, 0), (2, 3), (3, 2)]
INNER = [(1, 2), (2, 1)]


def inner_swap(value):
    groups = lax.axis_size("hg")
    pairs = [(a * groups + h, b * groups + h) for a, b in line_pairs(INNER) for h in range(groups)]
    pairs += [(a * groups + h, a * groups + (h ^ 1)) for a, _ in line_pairs([(0, 0), (3, 3)]) for h in range(groups)]
    return lax.ppermute(value, ("ctx", "hg"), pairs)


def line_groups(line):
    return [[2 * i + y for i in range(line)] for y in range(2)]


def after(value, *others):
    return lax.optimization_barrier((value, *others))[0] if others else value


def tie(value, name, default, **named):
    return after(value, *[named[n] for n in OPT.get(name, default).split() if n in named])


def body(doc_ids, rotated_queries, rotated_keys, value_matrix, out_proj, cotangent):
    rows = rotated_queries.shape[0]
    columns = rotated_queries.shape[1]
    shard = out_proj.shape[0]
    devices = lax.axis_size("ctx")
    groups = lax.axis_size("hg")
    line = devices // 2
    index = lax.axis_index("ctx")
    parity, place = index % 2, index // 2
    group = lax.axis_index("hg")

    kv = jnp.concatenate([rotated_keys, value_matrix], 1)
    docs = jnp.pad(doc_ids.reshape(-1, 2 * HEAD_SIZE), ((0, DOC_ROWS - rows // (2 * HEAD_SIZE)), (0, 0)))
    pack = jnp.concatenate([kv, docs.astype(jnp.bfloat16)], 0)
    far_kv = shift_line(pack, 1)

    fast = line == 4 and groups == 4 and shard % HEAD_SIZE == 0
    low = place < 2
    order = [jnp.where(low, 3, 0), jnp.where(low, 2, 1), place ^ 1, place] if fast else list(range(line))
    part = rows // groups

    def columns_of(value, row, count, kind):
        return jnp.concatenate([
            lax.dynamic_slice(value, (row, (2 * order[i] + kind) * shard), (count, shard)) for i in range(line)
        ], 1)

    cotangent = after(cotangent, pack)
    sent = columns_of(cotangent, group * part, part, 1 - parity)
    out_proj = tie(out_proj, "w", "sent", sent=sent, pack=pack)
    quarter = swap_pair(sent)
    blocks = columns_of(after(cotangent, sent), 0, rows, parity)
    relay = jnp.where(parity == 0, pack, after(far_kv, blocks))
    near_kv = swap_pair(relay)

    def docs_of(received, back):
        found = received[rows : rows + rows // (2 * HEAD_SIZE)].reshape(-1).astype(jnp.int32)
        return jnp.where(index >= back, found, -1)

    doc_window = jnp.concatenate([docs_of(far_kv, 2), docs_of(near_kv, 1), doc_ids])
    start = jnp.sum((doc_window[:, None] < doc_ids[None, :]).astype(jnp.int32), axis=0, keepdims=True)

    if fast:
        first = along_line(out_proj, OUTER)
        second = inner_swap(out_proj)
        quarter = after(quarter, relay)
        first, second = after(first, quarter), after(second, quarter)
        near_kv = tie(near_kv, "attend", "first second", first=first, second=second)
        third = inner_swap(first)
        fourth = along_line(second, OUTER)
        end = (place == 0) | (place == 3)
    else:
        weights = lax.all_gather(out_proj, "ctx", axis=0, axis_index_groups=line_groups(line)).reshape(-1, columns)

    attended, log_total = attend(start, rotated_queries, far_kv, near_kv, rotated_keys, value_matrix)
    pair_attended = swap_pair(attended)

    own_proj = dot_tn(blocks, attended)
    across = swap_heads(quarter, 2)
    if fast:
        third = tie(third, "fifth", "attended", attended=attended, own_proj=own_proj, across=across, log=log_total)
        fifth = along_line(third, OUTER)
        across = tie(across, "mates", "attended", attended=attended, third=third, own_proj=own_proj)
    mates = [swap_heads(quarter, 1), swap_heads(across, 1)]
    pair_blocks = jnp.zeros_like(blocks)
    for piece, owner in ((quarter, group), (mates[0], group ^ 1), (across, group ^ 2), (mates[1], group ^ 3)):
        pair_blocks = lax.dynamic_update_slice(pair_blocks, piece, (owner * part, 0))

    ways = [group ^ 3, group ^ 1, group ^ 2, group]

    if fast:
        near_half = jnp.concatenate([first, out_proj], 0)
        near_part = dot_nn(pair_blocks[:, 2 * shard :], near_half)
        if OPT.get("ownearly", 0):
            own_near = dot_nn(blocks[:, 2 * shard :], near_half)
            pair_attended = after(pair_attended, own_near)
        pair_attended = tie(pair_attended, "pa", "own_proj near_part", own_proj=own_proj, near_part=near_part)
        parts = [(own_proj[:shard] + dot_tn(pair_blocks[:, :shard], pair_attended)).astype(jnp.bfloat16)]
        farthest = along_line(parts[0], OUTER)
        fifth = tie(fifth, "far", "part0", part0=parts[0])
        far_half = jnp.concatenate([jnp.where(end, fifth, third), jnp.where(end, fourth, second)], 0)
        pair_part = (dot_nn(pair_blocks[:, : 2 * shard], far_half) + near_part).astype(jnp.bfloat16)
        if OPT.get("wbar", 1):
            far_half, pair_attended = lax.optimization_barrier((far_half, pair_attended, pair_part))[0:2]
        pair_part = swap_pair(pair_part)

        late_attended = tie(pair_attended, "chunks", "", far_half=far_half)
        parts.append(
            (own_proj[shard:] + dot_tn(pair_blocks[:, shard:], late_attended)).astype(jnp.bfloat16)
        )
        wide = [part.astype(jnp.float32) for part in (parts[0], parts[1][:shard], parts[1][shard : 2 * shard], parts[1][2 * shard :])]
        farther = along_line(parts[1][:shard], OUTER)
        core, column = group % 2, group // 2
        slots = [
            jnp.where(place % 2 == core, 1, 0),
            jnp.where(low == (core == 1), 0, 1),
            jnp.where(low == (column == 1), 0, 1),
        ]
        slots = jnp.stack(slots).astype(jnp.int32)
        if OPT.get("ownearly", 0):
            own_part = own_near + dot_nn(blocks[:, : 2 * shard], far_half)
        else:
            own_part = dot_nn(blocks[:, 2 * shard :], near_half) + dot_nn(blocks[:, : 2 * shard], far_half)
        inner = (wide[0] + farthest).astype(jnp.bfloat16)

        def across_of(tokens):
            sent, kept = output_parts_of(slots, tokens, far_half, near_half)
            mate = swap_heads(sent, 1)
            return (kept[0].astype(jnp.float32) + mate[0]).astype(jnp.bfloat16), kept[1].astype(jnp.float32), mate[1]

        sums = [across_of(pair_attended)]
        sums.append(across_of(tie(attended, "out1", "", inner=inner, sent0=sums[0][0], own=own_part)))
        sent1 = tie(sums[1][0], "sent1", "sent0", sent0=sums[0][0])
        pair_part = tie(pair_part, "bwd", "inner sent0 sent1", inner=inner, sent0=sums[0][0], sent1=sent1)
        inner = jnp.where(end, 0, inner_swap(inner))
        reduced = [
            (near + mate + swap_heads(sent, 2)).astype(jnp.bfloat16)
            for sent, near, mate in ((sums[0][0], *sums[0][1:]), (sent1, *sums[1][1:]))
        ]
    else:
        proj_parts = (own_proj + dot_tn(pair_blocks, pair_attended)).astype(jnp.bfloat16)
        proj_parts = proj_parts.reshape(line, shard, columns)
        proj_grad = lax.psum_scatter(proj_parts, "ctx", scatter_dimension=0, axis_index_groups=line_groups(line))
        pair_part = swap_pair(dot_nn(pair_blocks, weights).astype(jnp.bfloat16))
        own_part = dot_nn(blocks, weights)
        chunks = weights.reshape(groups, -1, columns)
        items = [lax.dynamic_index_in_dim(chunks, way, 0, keepdims=False) for way in ways]
        reduced = []
        for tokens in (pair_attended, attended):
            parts = [dot_nt(tokens, item) for item in items]
            mates = swap_heads(jnp.stack(parts[0:2]).astype(jnp.bfloat16), 1)
            across = swap_heads((parts[2] + mates[0]).astype(jnp.bfloat16), 2)
            reduced.append((parts[3] + mates[1] + across).astype(jnp.bfloat16))

    query_grad, near, far, own = attend_back(
        start, log_total, rotated_queries, far_kv, near_kv, rotated_keys, value_matrix, attended, own_part, pair_part
    )
    returned = swap_pair(near)
    if fast:
        returned = tie(returned, "returned", "red0", red0=reduced[0], red1=reduced[1])
    passed = far.astype(jnp.float32) + jnp.where(parity == 1, returned, 0)
    passed = passed.astype(jnp.bfloat16)
    if fast:
        wide[2] = tie(wide[2], "nearer", "own", own=own, passed=passed)
        nearer = (wide[2] + inner).astype(jnp.bfloat16)
        wide[1] = tie(wide[1], "other", "own", own=own, passed=passed, nearer=nearer)
        other = (wide[1] + farther).astype(jnp.bfloat16)
        passed = tie(passed, "passed", "", nearer=nearer, other=other)
        nearer = along_line(nearer, OUTER)
        other = jnp.where(end, 0, inner_swap(other))
        proj_grad = (wide[3] + nearer + other).astype(jnp.bfloat16)
    other_output, own_output = swap_pair(reduced[0]), reduced[1]
    if own_output.shape[1] == shard:
        layer_output = jnp.zeros((rows, 2 * shard), own_output.dtype)
        layer_output = lax.dynamic_update_slice(layer_output, own_output, (0, parity * shard))
        if OPT.get("asm", 1):
            other_output = after(other_output, layer_output)
        layer_output = lax.dynamic_update_slice(layer_output, other_output, (0, (1 - parity) * shard))
    else:
        halves = [jnp.where(parity == 0, own_output, other_output), jnp.where(parity == 0, other_output, own_output)]
        layer_output = jnp.stack([half.reshape(rows, -1, shard) for half in halves], 2).reshape(rows, -1)

    arrived = shift_line(passed, -1)
    own = own + jnp.where(place < line - 1, arrived, 0) + jnp.where(parity == 0, returned, 0)
    own = own.astype(jnp.bfloat16)
    return (layer_output, query_grad, own[:, 0:HEAD_SIZE], own[:, HEAD_SIZE:], proj_grad)


def solution(mesh):
    split = P("ctx", "hg")
    in_specs = (P("ctx"), split, split, split, split, P("ctx", None))
    return jax.shard_map(body, mesh=mesh, in_specs=in_specs, out_specs=(split,) * 5, check_vma=False)
```

```python
import functools

import functools

import jax
import jax.numpy as jnp
from jax import lax
from jax.experimental import pallas as pl
from jax.experimental.pallas import tpu as pltpu
from jax.sharding import PartitionSpec as P

HEAD_SIZE = 128
DOC_MOST = 1024
QUERY_TILE = 256
SCALE = HEAD_SIZE**-0.5
LOG2E = 1.4426950408889634
DOC_ROWS = 16


def dot_nn(a, b):
    return lax.dot_general(a, b, (((1,), (0,)), ((), ())), preferred_element_type=jnp.float32)


def dot_nt(a, b):
    return lax.dot_general(a, b, (((1,), (1,)), ((), ())), preferred_element_type=jnp.float32)


def dot_tn(a, b):
    return lax.dot_general(a, b, (((0,), (0,)), ((), ())), preferred_element_type=jnp.float32)


def windows(rows, key_rows):
    tile = min(QUERY_TILE, rows)
    for first in range(0, rows, tile):
        yield first, tile, first, DOC_MOST + tile


def mask_of(start_row, first, tile, low, width):
    key_pos = lax.broadcasted_iota(jnp.int32, (width, tile), 0) + low
    query_pos = lax.broadcasted_iota(jnp.int32, (width, tile), 1) + (first + DOC_MOST)
    return (key_pos <= query_pos) & (key_pos >= start_row)


def fill_keys(kv2, kv1, key_ref, value_ref, keys, values, rows):
    keys[0:rows] = kv2[0:rows, 0:HEAD_SIZE]
    keys[rows : 2 * rows] = kv1[0:rows, 0:HEAD_SIZE]
    keys[2 * rows : 3 * rows] = key_ref[...]
    values[0:rows] = kv2[0:rows, HEAD_SIZE:]
    values[rows : 2 * rows] = kv1[0:rows, HEAD_SIZE:]
    values[2 * rows : 3 * rows] = value_ref[...]


def forward_kernel(start, query, kv2, kv1, key_ref, value_ref, attended, log_total, keys, values):
    rows = query.shape[0]
    heads = query.shape[1] // HEAD_SIZE
    fill_keys(kv2, kv1, key_ref, value_ref, keys, values, rows)
    values_t = values[...].T
    for first, tile, low, width in windows(rows, keys.shape[0]):
        allowed = mask_of(start[:, first : first + tile], first, tile, low, width)
        for head in range(heads):
            lanes = slice(head * HEAD_SIZE, (head + 1) * HEAD_SIZE)
            scores = dot_nt(keys[low : low + width], query[first : first + tile, lanes])
            scores = jnp.where(allowed, scores * (SCALE * LOG2E), -jnp.inf)
            most = jnp.max(scores, axis=0, keepdims=True)
            weights = jnp.exp2(scores - most)
            weights = weights.astype(jnp.bfloat16)
            out = dot_nn(values_t[:, low : low + width], weights)
            total = dot_nn(jnp.ones((8, width), jnp.bfloat16), weights)[0:1]
            attended[first : first + tile, lanes] = (out / total).T.astype(jnp.bfloat16)
            log_total[head : head + 1, first : first + tile] = most + jnp.log2(total)


def backward_kernel(
    halo, start, log_total, query, kv2, kv1, key_ref, value_ref, attended, own_grad, pair_grad, *rest
):
    rows = query.shape[0]
    heads = query.shape[1] // HEAD_SIZE
    if halo:
        partial, near, far, keys, values, key_sum, value_sum, grad = rest
    else:
        partial, query_grad, own, keys, values, key_sum, value_sum, grad = rest
    fill_keys(kv2, kv1, key_ref, value_ref, keys, values, rows)
    keys_t = keys[...].T
    grad[...] = (own_grad[...] + pair_grad[...]).astype(grad.dtype)
    key_sum[...] = jnp.zeros_like(key_sum)
    value_sum[...] = jnp.zeros_like(value_sum)
    for first, tile, low, width in windows(rows, keys.shape[0]):
        if halo:
            width = DOC_MOST - low
        else:
            low, width = DOC_MOST, low + width - DOC_MOST
        allowed = mask_of(start[:, first : first + tile], first, tile, low, width)
        for head in range(heads):
            lanes = slice(head * HEAD_SIZE, (head + 1) * HEAD_SIZE)
            query_head = query[first : first + tile, lanes]
            grad_head = grad[first : first + tile, lanes]
            out_head = attended[first : first + tile, lanes]
            scores = dot_nt(keys[low : low + width], query_head) * (SCALE * LOG2E)
            scores = scores - log_total[head : head + 1, first : first + tile]
            weights = jnp.where(allowed, jnp.exp2(scores), 0.0)
            delta = grad_head.astype(jnp.float32) * out_head.astype(jnp.float32)
            delta = jnp.sum(delta.T, axis=0, keepdims=True)
            grad_dots = dot_nt(values[low : low + width], grad_head)
            shifted = (weights * (grad_dots - delta)).astype(jnp.bfloat16)
            value_sum[low : low + width] += dot_nn(weights.astype(jnp.bfloat16), grad_head)
            key_sum[low : low + width] += dot_nn(shifted, query_head)
            back = dot_nn(keys_t[:, low : low + width], shifted) * SCALE
            if halo:
                partial[lanes, first : first + tile] = back
            else:
                back += partial[lanes, first : first + tile]
                query_grad[first : first + tile, lanes] = back.T.astype(jnp.bfloat16)
    for place, out in ((0, far), (1, near)) if halo else ((2, own),):
        part = slice(place * rows, (place + 1) * rows)
        out[:, 0:HEAD_SIZE] = (key_sum[part] * SCALE).astype(out.dtype)
        out[:, HEAD_SIZE:] = value_sum[part].astype(out.dtype)


def whole_vmem(count):
    return [pl.BlockSpec(memory_space=pltpu.VMEM)] * count


def params(megabytes):
    return pltpu.CompilerParams(vmem_limit_bytes=megabytes * 1024 * 1024)


def attend(start, query, kv2, kv1, key, value):
    rows, columns = query.shape
    heads = columns // HEAD_SIZE
    cost = rows * (DOC_MOST + rows) * heads
    return pl.pallas_call(
        forward_kernel,
        out_shape=(
            jax.ShapeDtypeStruct((rows, columns), jnp.bfloat16),
            jax.ShapeDtypeStruct((heads, rows), jnp.float32),
        ),
        in_specs=whole_vmem(6),
        out_specs=tuple(whole_vmem(2)),
        scratch_shapes=[pltpu.VMEM((3 * rows, HEAD_SIZE), jnp.bfloat16)] * 2,
        compiler_params=params(16),
        cost_estimate=pl.CostEstimate(flops=cost * 512, transcendentals=cost, bytes_accessed=4 * rows * columns),
        name="attend",
    )(start, query, kv2, kv1, key, value)


def attend_back(halo, start, log_total, query, *others):
    rows, columns = query.shape
    heads = columns // HEAD_SIZE
    cost = rows * (DOC_MOST + rows) * heads // 2
    pair = jax.ShapeDtypeStruct((rows, 2 * HEAD_SIZE), jnp.bfloat16)
    result = jax.ShapeDtypeStruct((rows, columns), jnp.bfloat16)
    own = jax.ShapeDtypeStruct((rows, 2 * HEAD_SIZE), jnp.float32)
    if halo:
        outs = (jax.ShapeDtypeStruct((columns, rows), jnp.float32), pair, pair)
    else:
        outs = (result, own)
    return pl.pallas_call(
        functools.partial(backward_kernel, halo),
        out_shape=outs,
        in_specs=whole_vmem(3 + len(others)),
        out_specs=tuple(whole_vmem(len(outs))),
        scratch_shapes=[pltpu.VMEM((3 * rows, HEAD_SIZE), jnp.bfloat16)] * 2
        + [pltpu.VMEM((3 * rows, HEAD_SIZE), jnp.float32)] * 2
        + [pltpu.VMEM((rows, columns), jnp.bfloat16)],
        compiler_params=params(24),
        cost_estimate=pl.CostEstimate(flops=cost * 1280, transcendentals=cost, bytes_accessed=10 * rows * columns),
        name="attend_back_halo" if halo else "attend_back_own",
    )(start, log_total, query, *others)


def output_kernel(slots, tokens, late, early, sent, kept):
    shard = sent.shape[2]
    for weights, own, role in ((early, slots[0], slots[2]), (late, slots[1], 1 - slots[2])):
        for row, out in ((1 - own, sent), (own, kept)):
            rows = pl.ds(pl.multiple_of(row * shard, shard), shard)
            out[role] = dot_nt(tokens[...], weights[rows]).astype(out.dtype)


def output_parts_of(slots, tokens, late, early):
    shard, columns = early.shape[0] // 2, early.shape[1]
    rows = tokens.shape[0]
    result = jax.ShapeDtypeStruct((2, rows, shard), jnp.bfloat16)
    return pl.pallas_call(
        output_kernel,
        out_shape=(result, result),
        in_specs=[pl.BlockSpec(memory_space=pltpu.SMEM)] + whole_vmem(3),
        out_specs=tuple(whole_vmem(2)),
        compiler_params=params(12),
        cost_estimate=pl.CostEstimate(
            flops=8 * shard * rows * columns, transcendentals=0, bytes_accessed=32 * shard * rows
        ),
        name="output_parts",
    )(slots, tokens, late, early)


def swap_pair(value):
    devices = lax.axis_size("ctx")
    return lax.ppermute(value, "ctx", [(i, i ^ 1) for i in range(devices)])


def shift_line(value, by):
    devices = lax.axis_size("ctx")
    return lax.ppermute(value, "ctx", [(i, (i + 2 * by) % devices) for i in range(devices)])


def swap_heads(value, bit):
    groups = lax.axis_size("hg")
    return lax.ppermute(value, "hg", [(i, i ^ bit) for i in range(groups)])


def line_pairs(pairs):
    return [(2 * a + y, 2 * b + y) for a, b in pairs for y in range(2)]


def along_line(value, pairs):
    return lax.ppermute(value, "ctx", line_pairs(pairs))


OUTER = [(0, 1), (1, 0), (2, 3), (3, 2)]
OUTWARD = [(1, 0), (2, 3)]
INWARD = [(0, 1), (3, 2)]
INNER = [(1, 2), (2, 1)]


def inner_swap(value):
    groups = lax.axis_size("hg")
    pairs = [(a * groups + h, b * groups + h) for a, b in line_pairs(INNER) for h in range(groups)]
    pairs += [(a * groups + h, a * groups + (h ^ 1)) for a, _ in line_pairs([(0, 0), (3, 3)]) for h in range(groups)]
    return lax.ppermute(value, ("ctx", "hg"), pairs)


def line_groups(line):
    return [[2 * i + y for i in range(line)] for y in range(2)]


def after(value, *others):
    return lax.optimization_barrier((value, *others))[0]


def body(doc_ids, rotated_queries, rotated_keys, value_matrix, out_proj, cotangent):
    rows = rotated_queries.shape[0]
    columns = rotated_queries.shape[1]
    shard = out_proj.shape[0]
    devices = lax.axis_size("ctx")
    groups = lax.axis_size("hg")
    line = devices // 2
    index = lax.axis_index("ctx")
    parity, place = index % 2, index // 2
    group = lax.axis_index("hg")

    doc_rows = rows // HEAD_SIZE
    docs = jnp.pad(doc_ids.reshape(doc_rows, HEAD_SIZE), ((0, DOC_ROWS - doc_rows), (0, HEAD_SIZE))).astype(jnp.bfloat16)
    pack = jnp.concatenate([jnp.concatenate([rotated_keys, value_matrix], 1), docs], 0)
    far_kv = shift_line(pack, 1)

    fast = line == 4 and groups == 4 and shard % HEAD_SIZE == 0
    low = place < 2
    order = [jnp.where(low, 3, 0), jnp.where(low, 2, 1), place ^ 1, place] if fast else list(range(line))
    part = rows // groups

    def columns_of(value, row, count, kind):
        return jnp.concatenate([
            lax.dynamic_slice(value, (row, (2 * order[i] + kind) * shard), (count, shard)) for i in range(line)
        ], 1)

    cotangent = after(cotangent, pack)
    sent = columns_of(cotangent, group * part, part, 1 - parity)
    out_proj = after(out_proj, sent)
    quarter = swap_pair(sent)
    blocks = columns_of(after(cotangent, sent), 0, rows, parity)
    relay = jnp.where(parity == 0, pack, after(far_kv, blocks))
    near_kv = swap_pair(relay)

    def docs_of(received, back):
        found = received[rows : rows + doc_rows, :HEAD_SIZE].astype(jnp.int32).reshape(-1)
        return jnp.where(index >= back, found, -1)

    doc_window = jnp.concatenate([docs_of(far_kv, 2), docs_of(near_kv, 1), doc_ids])
    start = jnp.sum((doc_window[:, None] < doc_ids[None, :]).astype(jnp.int32), axis=0, keepdims=True)

    if fast:
        first, second = along_line(out_proj, OUTER), inner_swap(out_proj)
        quarter = after(quarter, relay)
        first, second = after(first, quarter), after(second, quarter)
        near_kv = after(near_kv, first, second)
        third, fourth = inner_swap(first), along_line(second, OUTER)
        end = (place == 0) | (place == 3)
    else:
        weights = lax.all_gather(out_proj, "ctx", axis=0, axis_index_groups=line_groups(line)).reshape(-1, columns)

    attended, log_total = attend(start, rotated_queries, far_kv, near_kv, rotated_keys, value_matrix)
    pair_attended = swap_pair(attended)

    own_proj = dot_tn(blocks, attended)
    across = swap_heads(quarter, 2)
    if fast:
        fifth = along_line(after(third, attended), OUTWARD)
    mates = [swap_heads(quarter, 1), swap_heads(across, 1)]
    pair_blocks = jnp.zeros_like(blocks)
    for piece, owner in ((quarter, group), (mates[0], group ^ 1), (across, group ^ 2), (mates[1], group ^ 3)):
        pair_blocks = lax.dynamic_update_slice(pair_blocks, piece, (owner * part, 0))

    ways = [group ^ 3, group ^ 1, group ^ 2, group]

    if fast:
        near_half = jnp.concatenate([first, out_proj], 0)
        near_part = dot_nn(pair_blocks[:, 2 * shard :], near_half)
        own_near = dot_nn(blocks[:, 2 * shard :], near_half)
        pair_attended = after(pair_attended, own_near)
        parts = [(own_proj[:shard] + dot_tn(pair_blocks[:, :shard], pair_attended)).astype(jnp.bfloat16)]
        farthest = along_line(parts[0], INWARD)
        fifth = after(fifth, parts[0])
        far_half = jnp.concatenate([jnp.where(end, fifth, third), jnp.where(end, fourth, second)], 0)
        pair_part = (dot_nn(pair_blocks[:, : 2 * shard], far_half) + near_part).astype(jnp.bfloat16)
        far_half, pair_attended = lax.optimization_barrier((far_half, pair_attended, pair_part))[0:2]
        pair_part = swap_pair(pair_part)

        late_attended = after(pair_attended, far_half)
        parts.append(
            (own_proj[shard:] + dot_tn(pair_blocks[:, shard:], late_attended)).astype(jnp.bfloat16)
        )
        wide = [part.astype(jnp.float32) for part in (parts[0], parts[1][:shard], parts[1][shard : 2 * shard], parts[1][2 * shard :])]
        farther = along_line(parts[1][:shard], OUTER)
        core, column = group % 2, group // 2
        slots = [
            jnp.where(place % 2 == core, 1, 0),
            jnp.where(low == (core == 1), 0, 1),
            jnp.where(low == (column == 1), 0, 1),
        ]
        slots = jnp.stack(slots).astype(jnp.int32)
        own_part = own_near + dot_nn(blocks[:, : 2 * shard], far_half)
        inner = (wide[0] + farthest).astype(jnp.bfloat16)

        def across_of(tokens):
            sent, kept = output_parts_of(slots, tokens, far_half, near_half)
            mate = swap_heads(sent, 1)
            return (kept[0].astype(jnp.float32) + mate[0]).astype(jnp.bfloat16), kept[1].astype(jnp.float32), mate[1]

        sums = [across_of(pair_attended)]
        sums.append(across_of(attended))
        sent1 = after(sums[1][0], sums[0][0])
        pair_part = after(pair_part, inner, sums[0][0])
        inner = jnp.where(end, 0, inner_swap(inner))
        reduced = [
            (near + mate + swap_heads(sent, 2)).astype(jnp.bfloat16)
            for sent, near, mate in ((sums[0][0], *sums[0][1:]), (sent1, *sums[1][1:]))
        ]
    else:
        proj_parts = (own_proj + dot_tn(pair_blocks, pair_attended)).astype(jnp.bfloat16)
        proj_parts = proj_parts.reshape(line, shard, columns)
        proj_grad = lax.psum_scatter(proj_parts, "ctx", scatter_dimension=0, axis_index_groups=line_groups(line))
        pair_part = swap_pair(dot_nn(pair_blocks, weights).astype(jnp.bfloat16))
        own_part = dot_nn(blocks, weights)
        chunks = weights.reshape(groups, -1, columns)
        items = [lax.dynamic_index_in_dim(chunks, way, 0, keepdims=False) for way in ways]
        reduced = []
        for tokens in (pair_attended, attended):
            parts = [dot_nt(tokens, item) for item in items]
            mates = swap_heads(jnp.stack(parts[0:2]).astype(jnp.bfloat16), 1)
            across = swap_heads((parts[2] + mates[0]).astype(jnp.bfloat16), 2)
            reduced.append((parts[3] + mates[1] + across).astype(jnp.bfloat16))

    operands = (start, log_total, rotated_queries, far_kv, near_kv, rotated_keys, value_matrix, attended, own_part, pair_part)
    partial, near, far = attend_back(True, *operands)
    query_grad, own = attend_back(False, *operands, partial)
    returned = swap_pair(near)
    if fast:
        returned = after(returned, reduced[0])
    passed = far.astype(jnp.float32) + jnp.where(parity == 1, returned, 0)
    passed = passed.astype(jnp.bfloat16)
    if fast:
        wide[2] = after(wide[2], own)
        nearer = (wide[2] + inner).astype(jnp.bfloat16)
        wide[1] = after(wide[1], own)
        other = (wide[1] + farther).astype(jnp.bfloat16)
        nearer = along_line(nearer, OUTER)
        other = jnp.where(end, 0, inner_swap(other))
        proj_grad = (wide[3] + nearer + other).astype(jnp.bfloat16)
    other_output, own_output = swap_pair(reduced[0]), reduced[1]
    if own_output.shape[1] == shard:
        layer_output = jnp.zeros((rows, 2 * shard), own_output.dtype)
        layer_output = lax.dynamic_update_slice(layer_output, own_output, (0, parity * shard))
        other_output = after(other_output, layer_output)
        layer_output = lax.dynamic_update_slice(layer_output, other_output, (0, (1 - parity) * shard))
    else:
        halves = [jnp.where(parity == 0, own_output, other_output), jnp.where(parity == 0, other_output, own_output)]
        layer_output = jnp.stack([half.reshape(rows, -1, shard) for half in halves], 2).reshape(rows, -1)

    arrived = shift_line(passed, -1)
    own = own + jnp.where(place < line - 1, arrived, 0) + jnp.where(parity == 0, returned, 0)
    own = own.astype(jnp.bfloat16)
    return (layer_output, query_grad, own[:, 0:HEAD_SIZE], own[:, HEAD_SIZE:], proj_grad)


def solution(mesh):
    split = P("ctx", "hg")
    in_specs = (P("ctx"), split, split, split, split, P("ctx", None))
    return jax.shard_map(body, mesh=mesh, in_specs=in_specs, out_specs=(split,) * 5, check_vma=False)
```

```python
import functools

import functools

import jax
import jax.numpy as jnp
from jax import lax
from jax.experimental import pallas as pl
from jax.experimental.pallas import tpu as pltpu
from jax.sharding import PartitionSpec as P

HEAD_SIZE = 128
DOC_MOST = 1024
QUERY_TILE = 256
SCALE = HEAD_SIZE**-0.5
LOG2E = 1.4426950408889634
DOC_ROWS = 16


def dot_nn(a, b):
    return lax.dot_general(a, b, (((1,), (0,)), ((), ())), preferred_element_type=jnp.float32)


def dot_nt(a, b):
    return lax.dot_general(a, b, (((1,), (1,)), ((), ())), preferred_element_type=jnp.float32)


def dot_tn(a, b):
    return lax.dot_general(a, b, (((0,), (0,)), ((), ())), preferred_element_type=jnp.float32)


def windows(rows, key_rows):
    tile = min(QUERY_TILE, rows)
    for first in range(0, rows, tile):
        yield first, tile, first, DOC_MOST + tile


def mask_of(start_row, first, tile, low, width):
    key_pos = lax.broadcasted_iota(jnp.int32, (width, tile), 0) + low
    query_pos = lax.broadcasted_iota(jnp.int32, (width, tile), 1) + (first + DOC_MOST)
    return (key_pos <= query_pos) & (key_pos >= start_row)


def fill_keys(kv2, kv1, key_ref, value_ref, keys, values, rows):
    keys[0:rows] = kv2[0:rows, 0:HEAD_SIZE]
    keys[rows : 2 * rows] = kv1[0:rows, 0:HEAD_SIZE]
    keys[2 * rows : 3 * rows] = key_ref[...]
    values[0:rows] = kv2[0:rows, HEAD_SIZE:]
    values[rows : 2 * rows] = kv1[0:rows, HEAD_SIZE:]
    values[2 * rows : 3 * rows] = value_ref[...]


def forward_kernel(start, query, kv2, kv1, key_ref, value_ref, attended, log_total, keys, values):
    rows = query.shape[0]
    heads = query.shape[1] // HEAD_SIZE
    fill_keys(kv2, kv1, key_ref, value_ref, keys, values, rows)
    values_t = values[...].T
    for first, tile, low, width in windows(rows, keys.shape[0]):
        allowed = mask_of(start[:, first : first + tile], first, tile, low, width)
        for head in range(heads):
            lanes = slice(head * HEAD_SIZE, (head + 1) * HEAD_SIZE)
            scores = dot_nt(keys[low : low + width], query[first : first + tile, lanes])
            scores = jnp.where(allowed, scores * (SCALE * LOG2E), -jnp.inf)
            most = jnp.max(scores, axis=0, keepdims=True)
            weights = jnp.exp2(scores - most)
            weights = weights.astype(jnp.bfloat16)
            out = dot_nn(values_t[:, low : low + width], weights)
            total = dot_nn(jnp.ones((8, width), jnp.bfloat16), weights)[0:1]
            attended[first : first + tile, lanes] = (out / total).T.astype(jnp.bfloat16)
            log_total[head : head + 1, first : first + tile] = most + jnp.log2(total)


def backward_kernel(
    halo, start, log_total, query, kv2, kv1, key_ref, value_ref, attended, own_grad, pair_grad, *rest
):
    rows = query.shape[0]
    heads = query.shape[1] // HEAD_SIZE
    if halo:
        partial, near, far, keys, values, key_sum, value_sum, grad = rest
    else:
        partial, query_grad, own, keys, values, key_sum, value_sum, grad = rest
    fill_keys(kv2, kv1, key_ref, value_ref, keys, values, rows)
    keys_t = keys[...].T
    grad[...] = (own_grad[...] + pair_grad[...]).astype(grad.dtype)
    key_sum[...] = jnp.zeros_like(key_sum)
    value_sum[...] = jnp.zeros_like(value_sum)
    for first, tile, low, width in windows(rows, keys.shape[0]):
        if halo:
            width = DOC_MOST - low
        else:
            low, width = DOC_MOST, low + width - DOC_MOST
        allowed = mask_of(start[:, first : first + tile], first, tile, low, width)
        for head in range(heads):
            lanes = slice(head * HEAD_SIZE, (head + 1) * HEAD_SIZE)
            query_head = query[first : first + tile, lanes]
            grad_head = grad[first : first + tile, lanes]
            out_head = attended[first : first + tile, lanes]
            scores = dot_nt(keys[low : low + width], query_head) * (SCALE * LOG2E)
            scores = scores - log_total[head : head + 1, first : first + tile]
            weights = jnp.where(allowed, jnp.exp2(scores), 0.0)
            delta = grad_head.astype(jnp.float32) * out_head.astype(jnp.float32)
            delta = jnp.sum(delta.T, axis=0, keepdims=True)
            grad_dots = dot_nt(values[low : low + width], grad_head)
            shifted = (weights * (grad_dots - delta)).astype(jnp.bfloat16)
            value_sum[low : low + width] += dot_nn(weights.astype(jnp.bfloat16), grad_head)
            key_sum[low : low + width] += dot_nn(shifted, query_head)
            back = dot_nn(keys_t[:, low : low + width], shifted) * SCALE
            if halo:
                partial[lanes, first : first + tile] = back
            else:
                back += partial[lanes, first : first + tile]
                query_grad[first : first + tile, lanes] = back.T.astype(jnp.bfloat16)
    for place, out in ((0, far), (1, near)) if halo else ((2, own),):
        part = slice(place * rows, (place + 1) * rows)
        out[:, 0:HEAD_SIZE] = (key_sum[part] * SCALE).astype(out.dtype)
        out[:, HEAD_SIZE:] = value_sum[part].astype(out.dtype)


def whole_vmem(count):
    return [pl.BlockSpec(memory_space=pltpu.VMEM)] * count


def params(megabytes):
    return pltpu.CompilerParams(vmem_limit_bytes=megabytes * 1024 * 1024)


def attend(start, query, kv2, kv1, key, value):
    rows, columns = query.shape
    heads = columns // HEAD_SIZE
    cost = rows * (DOC_MOST + rows) * heads
    return pl.pallas_call(
        forward_kernel,
        out_shape=(
            jax.ShapeDtypeStruct((rows, columns), jnp.bfloat16),
            jax.ShapeDtypeStruct((heads, rows), jnp.float32),
        ),
        in_specs=whole_vmem(6),
        out_specs=tuple(whole_vmem(2)),
        scratch_shapes=[pltpu.VMEM((3 * rows, HEAD_SIZE), jnp.bfloat16)] * 2,
        compiler_params=params(16),
        cost_estimate=pl.CostEstimate(flops=cost * 512, transcendentals=cost, bytes_accessed=4 * rows * columns),
        name="attend",
    )(start, query, kv2, kv1, key, value)


def attend_back(halo, start, log_total, query, *others):
    rows, columns = query.shape
    heads = columns // HEAD_SIZE
    cost = rows * (DOC_MOST + rows) * heads // 2
    pair = jax.ShapeDtypeStruct((rows, 2 * HEAD_SIZE), jnp.bfloat16)
    result = jax.ShapeDtypeStruct((rows, columns), jnp.bfloat16)
    own = jax.ShapeDtypeStruct((rows, 2 * HEAD_SIZE), jnp.float32)
    if halo:
        outs = (jax.ShapeDtypeStruct((columns, rows), jnp.float32), pair, pair)
    else:
        outs = (result, own)
    return pl.pallas_call(
        functools.partial(backward_kernel, halo),
        out_shape=outs,
        in_specs=whole_vmem(3 + len(others)),
        out_specs=tuple(whole_vmem(len(outs))),
        scratch_shapes=[pltpu.VMEM((3 * rows, HEAD_SIZE), jnp.bfloat16)] * 2
        + [pltpu.VMEM((3 * rows, HEAD_SIZE), jnp.float32)] * 2
        + [pltpu.VMEM((rows, columns), jnp.bfloat16)],
        compiler_params=params(24),
        cost_estimate=pl.CostEstimate(flops=cost * 1280, transcendentals=cost, bytes_accessed=10 * rows * columns),
        name="attend_back_halo" if halo else "attend_back_own",
    )(start, log_total, query, *others)


def output_kernel(slots, tokens, late, early, sent, kept):
    shard = sent.shape[2]
    for weights, own, role in ((early, slots[0], slots[2]), (late, slots[1], 1 - slots[2])):
        for row, out in ((1 - own, sent), (own, kept)):
            rows = pl.ds(pl.multiple_of(row * shard, shard), shard)
            out[role] = dot_nt(tokens[...], weights[rows]).astype(out.dtype)


def output_parts_of(slots, tokens, late, early):
    shard, columns = early.shape[0] // 2, early.shape[1]
    rows = tokens.shape[0]
    result = jax.ShapeDtypeStruct((2, rows, shard), jnp.bfloat16)
    return pl.pallas_call(
        output_kernel,
        out_shape=(result, result),
        in_specs=[pl.BlockSpec(memory_space=pltpu.SMEM)] + whole_vmem(3),
        out_specs=tuple(whole_vmem(2)),
        compiler_params=params(12),
        cost_estimate=pl.CostEstimate(
            flops=8 * shard * rows * columns, transcendentals=0, bytes_accessed=32 * shard * rows
        ),
        name="output_parts",
    )(slots, tokens, late, early)


def swap_pair(value):
    devices = lax.axis_size("ctx")
    return lax.ppermute(value, "ctx", [(i, i ^ 1) for i in range(devices)])


def shift_line(value, by):
    devices = lax.axis_size("ctx")
    return lax.ppermute(value, "ctx", [(i, (i + 2 * by) % devices) for i in range(devices)])


def swap_heads(value, bit):
    groups = lax.axis_size("hg")
    return lax.ppermute(value, "hg", [(i, i ^ bit) for i in range(groups)])


def line_pairs(pairs):
    return [(2 * a + y, 2 * b + y) for a, b in pairs for y in range(2)]


def along_line(value, pairs):
    return lax.ppermute(value, "ctx", line_pairs(pairs))


OUTER = [(0, 1), (1, 0), (2, 3), (3, 2)]
OUTWARD = [(1, 0), (2, 3)]
INWARD = [(0, 1), (3, 2)]
INNER = [(1, 2), (2, 1)]


def inner_swap(value):
    groups = lax.axis_size("hg")
    pairs = [(a * groups + h, b * groups + h) for a, b in line_pairs(INNER) for h in range(groups)]
    pairs += [(a * groups + h, a * groups + (h ^ 1)) for a, _ in line_pairs([(0, 0), (3, 3)]) for h in range(groups)]
    return lax.ppermute(value, ("ctx", "hg"), pairs)


def line_groups(line):
    return [[2 * i + y for i in range(line)] for y in range(2)]


def after(value, *others):
    return lax.optimization_barrier((value, *others))[0]


def body(doc_ids, rotated_queries, rotated_keys, value_matrix, out_proj, cotangent):
    rows = rotated_queries.shape[0]
    columns = rotated_queries.shape[1]
    shard = out_proj.shape[0]
    devices = lax.axis_size("ctx")
    groups = lax.axis_size("hg")
    line = devices // 2
    index = lax.axis_index("ctx")
    parity, place = index % 2, index // 2
    group = lax.axis_index("hg")

    doc_rows = rows // HEAD_SIZE
    docs = jnp.pad(doc_ids.reshape(doc_rows, HEAD_SIZE), ((0, DOC_ROWS - doc_rows), (0, HEAD_SIZE))).astype(jnp.bfloat16)
    pack = jnp.concatenate([jnp.concatenate([rotated_keys, value_matrix], 1), docs], 0)
    far_kv = shift_line(pack, 1)

    fast = line == 4 and groups == 4 and shard % HEAD_SIZE == 0
    low = place < 2
    order = [jnp.where(low, 3, 0), jnp.where(low, 2, 1), place ^ 1, place] if fast else list(range(line))
    part = rows // groups

    def columns_of(value, row, count, kind):
        return jnp.concatenate([
            lax.dynamic_slice(value, (row, (2 * order[i] + kind) * shard), (count, shard)) for i in range(line)
        ], 1)

    cotangent = after(cotangent, pack)
    sent = columns_of(cotangent, group * part, part, 1 - parity)
    out_proj = after(out_proj, sent)
    quarter = swap_pair(sent)
    blocks = columns_of(after(cotangent, sent), 0, rows, parity)
    relay = jnp.where(parity == 0, pack, after(far_kv, blocks))
    near_kv = swap_pair(relay)

    def docs_of(received, back):
        found = received[rows : rows + doc_rows, :HEAD_SIZE].astype(jnp.int32).reshape(-1)
        return jnp.where(index >= back, found, -1)

    doc_window = jnp.concatenate([docs_of(far_kv, 2), docs_of(near_kv, 1), doc_ids])
    start = jnp.sum((doc_window[:, None] < doc_ids[None, :]).astype(jnp.int32), axis=0, keepdims=True)

    if fast:
        first, second = along_line(out_proj, OUTER), inner_swap(out_proj)
        quarter = after(quarter, relay)
        first, second = after(first, quarter), after(second, quarter)
        near_kv = after(near_kv, first, second)
        third, fourth = inner_swap(first), along_line(second, OUTER)
        end = (place == 0) | (place == 3)
    else:
        weights = lax.all_gather(out_proj, "ctx", axis=0, axis_index_groups=line_groups(line)).reshape(-1, columns)

    attended, log_total = attend(start, rotated_queries, far_kv, near_kv, rotated_keys, value_matrix)
    pair_attended = swap_pair(attended)

    own_proj = dot_tn(blocks, attended)
    across = swap_heads(quarter, 2)
    if fast:
        fifth = along_line(after(third, attended), OUTWARD)
    mates = [swap_heads(quarter, 1), swap_heads(across, 1)]
    pair_blocks = jnp.zeros_like(blocks)
    for piece, owner in ((quarter, group), (mates[0], group ^ 1), (across, group ^ 2), (mates[1], group ^ 3)):
        pair_blocks = lax.dynamic_update_slice(pair_blocks, piece, (owner * part, 0))

    ways = [group ^ 3, group ^ 1, group ^ 2, group]

    if fast:
        near_half = jnp.concatenate([first, out_proj], 0)
        near_part = dot_nn(pair_blocks[:, 2 * shard :], near_half)
        own_near = dot_nn(blocks[:, 2 * shard :], near_half)
        pair_attended = after(pair_attended, own_near)
        parts = [(own_proj[:shard] + dot_tn(pair_blocks[:, :shard], pair_attended)).astype(jnp.bfloat16)]
        farthest = along_line(parts[0], INWARD)
        fifth = after(fifth, parts[0])
        far_half = jnp.concatenate([jnp.where(end, fifth, third), jnp.where(end, fourth, second)], 0)
        pair_part = (dot_nn(pair_blocks[:, : 2 * shard], far_half) + near_part).astype(jnp.bfloat16)
        far_half, pair_attended = lax.optimization_barrier((far_half, pair_attended, pair_part))[0:2]
        pair_part = swap_pair(pair_part)

        late_attended = after(pair_attended, far_half)
        parts.append(
            (own_proj[shard:] + dot_tn(pair_blocks[:, shard:], late_attended)).astype(jnp.bfloat16)
        )
        wide = [part.astype(jnp.float32) for part in (parts[0], parts[1][:shard], parts[1][shard : 2 * shard], parts[1][2 * shard :])]
        farther = along_line(parts[1][:shard], OUTER)
        core, column = group % 2, group // 2
        slots = [
            jnp.where(place % 2 == core, 1, 0),
            jnp.where(low == (core == 1), 0, 1),
            jnp.where(low == (column == 1), 0, 1),
        ]
        slots = jnp.stack(slots).astype(jnp.int32)
        own_part = own_near + dot_nn(blocks[:, : 2 * shard], far_half)
        inner = (wide[0] + farthest).astype(jnp.bfloat16)

        def across_of(tokens):
            sent, kept = output_parts_of(slots, tokens, far_half, near_half)
            mate = swap_heads(sent, 1)
            return (kept[0].astype(jnp.float32) + mate[0]).astype(jnp.bfloat16), kept[1].astype(jnp.float32), mate[1]

        sums = [across_of(pair_attended)]
        sums.append(across_of(attended))
        sent1 = after(sums[1][0], sums[0][0])
        pair_part = after(pair_part, inner, sums[0][0])
        inner = jnp.where(end, 0, inner_swap(inner))
        reduced = [
            (near + mate + swap_heads(sent, 2)).astype(jnp.bfloat16)
            for sent, near, mate in ((sums[0][0], *sums[0][1:]), (sent1, *sums[1][1:]))
        ]
    else:
        proj_parts = (own_proj + dot_tn(pair_blocks, pair_attended)).astype(jnp.bfloat16)
        proj_parts = proj_parts.reshape(line, shard, columns)
        proj_grad = lax.psum_scatter(proj_parts, "ctx", scatter_dimension=0, axis_index_groups=line_groups(line))
        pair_part = swap_pair(dot_nn(pair_blocks, weights).astype(jnp.bfloat16))
        own_part = dot_nn(blocks, weights)
        chunks = weights.reshape(groups, -1, columns)
        items = [lax.dynamic_index_in_dim(chunks, way, 0, keepdims=False) for way in ways]
        reduced = []
        for tokens in (pair_attended, attended):
            parts = [dot_nt(tokens, item) for item in items]
            mates = swap_heads(jnp.stack(parts[0:2]).astype(jnp.bfloat16), 1)
            across = swap_heads((parts[2] + mates[0]).astype(jnp.bfloat16), 2)
            reduced.append((parts[3] + mates[1] + across).astype(jnp.bfloat16))

    operands = (start, log_total, rotated_queries, far_kv, near_kv, rotated_keys, value_matrix, attended, own_part, pair_part)
    partial, near, far = attend_back(True, *operands)
    query_grad, own = attend_back(False, *operands, partial)
    returned = swap_pair(near)
    if fast:
        returned = after(returned, reduced[0])
    passed = far.astype(jnp.float32) + jnp.where(parity == 1, returned, 0)
    passed = passed.astype(jnp.bfloat16)
    if fast:
        wide[2] = after(wide[2], own)
        nearer = (wide[2] + inner).astype(jnp.bfloat16)
        wide[1] = after(wide[1], own)
        other = (wide[1] + farther).astype(jnp.bfloat16)
        nearer = along_line(nearer, OUTER)
        other = jnp.where(end, 0, inner_swap(other))
        proj_grad = (wide[3] + nearer + other).astype(jnp.bfloat16)
    other_output, own_output = swap_pair(reduced[0]), reduced[1]
    halves = [jnp.where(parity == 0, own_output, other_output), jnp.where(parity == 0, other_output, own_output)]
    if own_output.shape[1] == shard:
        layer_output = jnp.concatenate(halves, 1)
    else:
        layer_output = jnp.stack([half.reshape(rows, -1, shard) for half in halves], 2).reshape(rows, -1)

    arrived = shift_line(passed, -1)
    own = own + jnp.where(place < line - 1, arrived, 0) + jnp.where(parity == 0, returned, 0)
    own = own.astype(jnp.bfloat16)
    return (layer_output, query_grad, own[:, 0:HEAD_SIZE], own[:, HEAD_SIZE:], proj_grad)


def solution(mesh):
    split = P("ctx", "hg")
    in_specs = (P("ctx"), split, split, split, split, P("ctx", None))
    return jax.shard_map(body, mesh=mesh, in_specs=in_specs, out_specs=(split,) * 5, check_vma=False)
```
